256 devices in a mesh: view: 4 (over y), frame: 16 (over x_hi, z), band: 4 (over x_lo, core).
Axes of the slice: x: 4 (x_hi: 2, x_lo: 2; x = x_hi * 2 + x_lo), y: 4, z: 8, core: 2. Of those that a mesh axis runs over, the one named last changes fastest.
Arguments:
- hidden: bfloat16 [4, 16, 32, 64, 1152], P('view', 'frame', 'band'), may hold values from -6 to 6
- cond_queries: bfloat16 [4, 16, 32, 64, 1152], P('view', 'frame', 'band')
- cond_kv: bfloat16 [4, 16, 32, 64, 2304], P('view', 'frame', 'band'), may hold values from -6 to 6
- layout_kv: bfloat16 [16, 512, 2304], P('frame', 'band')
- layout_count: int32 [16, 4], P('frame'), may hold values from 1 to 128, 320 in all within a row
- intersection: int32 [4, 2], P('view'), may hold values from 16 to 32
- norm_gain: float32 [1152], replicated, may hold values from 0.1 to 1.9
- w_qkv: bfloat16 [1152, 3456], replicated
Outputs:
- temporal_heads: bfloat16 [4, 16, 32, 64, 1152], P('view', 'frame', 'band')
The draws below stay inside these ranges and needn't reach their ends.
Inputs may be any that keep to these rules, and one draw needn't show every extreme that they name: `layout_count`: for each frame the counts sum to 320 and the largest is 128.
All inputs are finite; a program needn't handle non-finite values.
Results may differ from the reference program's by a relative error of at most 0.015.
Values may be sent and summed in bfloat16 or wider, within the bound.
No kernel may reach another device: no remote copies, remote signals or barrier semaphores. Data moves between devices by JAX's collectives and lax.ppermute only.
A program may use at most 192 MiB of HBM per device.

```python
import math
import jax
import jax.numpy as jnp
import numpy as np
from jax import lax

D = 1152
HEADS = 16
ROWS_DEV = 8
COLS = 64
LAY_DEV = 128
VIEWS = 4
FRAMES = 16
PROWS = 32
LAYOUT = 512
N_BAND = 4


def layout_base(key):
    return jax.random.normal(key, (FRAMES, LAYOUT, D), jnp.float32)


def draw_layout_kv(key, part):
    base = layout_base(key)
    key = jax.random.fold_in(key, 7)
    values_part = jax.random.normal(key, (FRAMES, LAYOUT, D), jnp.float32)
    keys_part = base
    return jnp.concatenate([keys_part, values_part], axis=-1).astype(jnp.bfloat16)


def draw_cond_queries(key, part):
    key = jax.random.fold_in(key, 5)
    queries = jax.random.normal(key, (VIEWS, FRAMES, PROWS, COLS, D), jnp.float32)
    return queries.astype(jnp.bfloat16)


def draw_w_qkv(key, part):
    key = jax.random.fold_in(key, 3)
    weights = jax.random.normal(key, (D, 3 * D), jnp.float32) / math.sqrt(D)
    return weights.astype(jnp.bfloat16)


def plant(drawn, key, smallest, high):
    longest = drawn.shape.index(max(drawn.shape))
    spots = []
    for shift in (0, 1):
        where = [jax.random.randint(jax.random.fold_in(key, axis), (), 0, length) for axis, length in enumerate(drawn.shape)]
        where[longest] = (where[longest] + shift) % drawn.shape[longest]
        spots.append(tuple(where))
    return drawn.at[spots[0]].set(smallest).at[spots[1]].set(high)


def block_scale(stream_key, dims, pieces, smallest, largest):
    factor_of, own = 1.0, jax.random.fold_in(stream_key, 6)
    for axis_at, shards_of in pieces:
        draws = jnp.exp(jax.random.uniform(jax.random.fold_in(own, axis_at), (shards_of,), jnp.float32, smallest / len(pieces), largest / len(pieces)))
        factor_of = factor_of * jnp.repeat(draws, dims[axis_at] // shards_of).reshape([-1 if axis == axis_at else 1 for axis in range(len(dims))])
    return factor_of


def profile(count, total, most, lean):
    portions = [(1 << 20) // math.isqrt(grade ** lean) + 1 for grade in range(2, count + 1)]
    rest, given = total - most - (count - 1), [1] * (count - 1)
    while rest > 0:
        candidates = [i for i in range(count - 1) if given[i] < most]
        whole, budget = sum([portions[i] for i in candidates]), rest
        for i in candidates:
            addition = min(most - given[i], max(1, budget * portions[i] // whole), rest)
            given[i] = given[i] + addition
            rest = rest - addition
    return np.array([most] + given)


def uneven_parts(stream_key, amount, total, most, skew):
    if amount == 2:
        one = jax.random.randint(stream_key, (), max(1, total - most), min(most, total - 1) + 1)
        return jnp.stack([one, total - one])
    sizes = jnp.asarray(profile(amount, total, most, skew), jnp.int32)
    couples = (amount - 1) // 2
    donor, sink = sizes[1:1 + 2 * couples:2], sizes[2:2 + 2 * couples:2]
    margin = jnp.minimum(donor - 1, most - sink)
    passed = jax.random.randint(jax.random.fold_in(stream_key, 1), (couples,), 0, 1 << 20) % (margin + 1)
    sizes = sizes.at[1:1 + 2 * couples:2].set(donor - passed).at[2:2 + 2 * couples:2].set(sink + passed)
    return sizes[jax.random.permutation(jax.random.fold_in(stream_key, 2), amount)]


def bell_draw(key, extent, spread, limit, pieces=(), kind=jnp.bfloat16):
    drawn = jax.random.normal(key, extent, jnp.float32) * spread
    if len(pieces) > 0:
        drawn = block_scale(key, extent, pieces, -0.22, 0.18) * drawn
    return jnp.clip(drawn, min=-limit, max=limit).astype(kind)


def setup_inputs(seed: int = 0) -> dict:
    key_list = jax.random.split(jax.random.key(seed), 9)
    hidden = bell_draw(key_list[0], (VIEWS, FRAMES, PROWS, COLS, D), 1.0, 6.0, ((0, 4), (1, 16), (2, 4)))
    cond_queries = draw_cond_queries(jax.random.fold_in(key_list[8], 71), 0)
    cond_kv = bell_draw(key_list[2], (VIEWS, FRAMES, PROWS, COLS, 2 * D), 1.0, 6.0, ((0, 4), (1, 16), (2, 4)))
    layout_kv = draw_layout_kv(jax.random.fold_in(key_list[8], 71), 0)
    layout_count = jax.vmap(lambda own: uneven_parts(own, N_BAND, 5 * LAYOUT // 8, LAY_DEV, 0))(jax.random.split(key_list[4], FRAMES)).reshape((FRAMES, N_BAND)).astype(jnp.int32)
    intersection = plant(jax.random.randint(key_list[5], (VIEWS, 2), COLS // 4, COLS // 2 + 1), jax.random.fold_in(key_list[5], 1), COLS // 4, (COLS // 2 + 1) - 1).astype(jnp.int32)
    norm_gain = jnp.clip(1.0 + 0.18 * jax.random.normal(key_list[6], (D,), jnp.float32), 0.1, 1.9)
    w_qkv = draw_w_qkv(jax.random.fold_in(key_list[8], 71), 0)
    return {"hidden": hidden, "cond_queries": cond_queries, "cond_kv": cond_kv, "layout_kv": layout_kv, "layout_count": layout_count, "intersection": intersection, "norm_gain": norm_gain, "w_qkv": w_qkv}


epsilon = 1e-06

def softmax_rows(scores):
    row_max = lax.optimization_barrier(jnp.max(scores, axis=-1, keepdims=True))
    exponent = jnp.exp(scores - row_max)
    return (exponent / lax.optimization_barrier(jnp.sum(exponent, axis=-1, keepdims=True))).astype(jnp.bfloat16)

def attend(queries, keys_values, key_live):
    model_width = queries.shape[-1]
    head_dim = model_width // HEADS
    key_count = keys_values.shape[0]
    query_heads = queries.reshape(-1, HEADS, head_dim).astype(jnp.float32)
    key_heads = keys_values[:, :model_width].reshape(key_count, HEADS, head_dim).astype(jnp.float32)
    value_heads = keys_values[:, model_width:].reshape(key_count, HEADS, head_dim).astype(jnp.float32)
    scores = jnp.einsum('qhe,khe->hqk', query_heads, key_heads) * (1.0 / math.sqrt(head_dim))
    scores = jnp.where(key_live[None, None, :], scores, -1e+30)
    weights = softmax_rows(scores)
    mixed_rows = jnp.einsum('hqk,khe->qhe', weights.astype(jnp.float32), value_heads)
    return mixed_rows.reshape(-1, model_width)

def temporal(packed):
    frame_count, positions = (packed.shape[0], packed.shape[1])
    model_width = packed.shape[2] // 3
    head_dim = model_width // HEADS
    query_heads = packed[:, :, :model_width].reshape(frame_count, positions, HEADS, head_dim).astype(jnp.float32)
    key_heads = packed[:, :, model_width:2 * model_width].reshape(frame_count, positions, HEADS, head_dim).astype(jnp.float32)
    value_heads = packed[:, :, 2 * model_width:].reshape(frame_count, positions, HEADS, head_dim).astype(jnp.float32)
    scores = jnp.einsum('fphe,gphe->phfg', query_heads, key_heads) * (1.0 / math.sqrt(head_dim))
    weights = softmax_rows(scores)
    result = jnp.einsum('phfg,gphe->fphe', weights.astype(jnp.float32), value_heads)
    return result.reshape(frame_count, positions, model_width).astype(jnp.bfloat16)

def project(state_rows, norm_gain, w_qkv):
    values_f = state_rows.astype(jnp.float32)
    inverse = lax.rsqrt(lax.optimization_barrier(jnp.mean(values_f * values_f, axis=-1, keepdims=True)) + epsilon)
    normed = (values_f * inverse * norm_gain).astype(jnp.bfloat16)
    return jnp.dot(normed, w_qkv, preferred_element_type=jnp.float32).astype(jnp.bfloat16)

def reference(hidden, cond_queries, cond_kv, layout_kv, layout_count, intersection, norm_gain, w_qkv):
    view_count = hidden.shape[0]
    half_cols = COLS // 2
    slot_index = jnp.arange(LAYOUT, dtype=jnp.int32)
    column = jnp.arange(half_cols, dtype=jnp.int32)

    def one_view(view_index):
        left_view = cond_kv[(view_index - 1) % view_count]
        right_view = cond_kv[(view_index + 1) % view_count]
        left_live = jnp.tile(column + half_cols >= COLS - intersection[view_index, 0], ROWS_DEV)
        right_live = jnp.tile(column < intersection[view_index, 1], ROWS_DEV)

        def one_frame(frame_index):
            slot_limit = layout_count[frame_index][slot_index // LAY_DEV]
            layout_live = slot_index % LAY_DEV < slot_limit
            queries = cond_queries[view_index, frame_index].reshape(N_BAND, ROWS_DEV * COLS, D)
            left_keys = left_view[frame_index][:, half_cols:, :].reshape(N_BAND, ROWS_DEV * half_cols, 2 * D)
            right_keys = right_view[frame_index][:, :half_cols, :].reshape(N_BAND, ROWS_DEV * half_cols, 2 * D)
            layout_rows = layout_kv[frame_index]

            def one_band(band_queries, band_left, band_right):
                keys_values = jnp.concatenate([band_left, band_right, layout_rows], axis=0)
                key_live = jnp.concatenate([left_live, right_live, layout_live])
                return attend(band_queries, keys_values, key_live)
            mixed_rows = jax.vmap(one_band)(queries, left_keys, right_keys)
            return mixed_rows.reshape(PROWS, COLS, D)
        mixed_view = lax.map(one_frame, jnp.arange(FRAMES, dtype=jnp.int32))
        state_rows = (hidden[view_index].astype(jnp.float32) + mixed_view).astype(jnp.bfloat16)
        packed = project(state_rows.reshape(-1, D), norm_gain, w_qkv)
        packed = packed.reshape(FRAMES, PROWS * COLS, 3 * D)
        return temporal(packed).reshape(FRAMES, PROWS, COLS, D)
    return lax.map(one_view, jnp.arange(view_count, dtype=jnp.int32))
```

```python
import functools
import math

import jax
import jax.numpy as jnp
from jax import lax
from jax.experimental import pallas as pl
from jax.experimental.pallas import tpu as pltpu
from jax.sharding import PartitionSpec as P

HEADS = 16
LANES = 128
CHUNKS = 2
EPSILON = 1e-06
DEAD = -1e30
VMEM_LIMIT = 56 << 20
LOG2E = 1.4426950408889634
NT = (((1,), (1,)), ((), ()))


def head_span(head, width):
    size = width // HEADS
    low, high = head * size, (head + 1) * size
    return low, high, low // LANES * LANES, -(-high // LANES) * LANES


def head_mask(head, rows, width):
    low, high, first, last = head_span(head, width)
    column = lax.broadcasted_iota(jnp.int32, (rows, last - first), 1) + first
    return (column >= low) & (column < high)


def row_max(pieces):
    return functools.reduce(
        jnp.maximum, [jnp.max(piece, axis=1, keepdims=True) for piece in pieces]
    )


def lane_index(count):
    return lax.broadcasted_iota(jnp.int32, (1, count), 1)


def layout_kernel(band_ref, count_ref, q_ref, *refs):
    blocks = [(refs[2 * i], refs[2 * i + 1]) for i in range(4)]
    acc_ref, max_ref, sum_ref = refs[8:]
    rows, width = q_ref.shape
    scale = LOG2E / math.sqrt(width // HEADS)
    band = band_ref[0]
    slots = blocks[0][0].shape[0]
    biases = []
    for i in range(4):
        limit = count_ref[0, jnp.bitwise_xor(band, i)]
        biases.append(jnp.where(lane_index(slots) < limit, 0.0, DEAD))
    done = 0
    for head in range(HEADS):
        low, high, first, last = head_span(head, width)
        mask = head_mask(head, rows, width)
        query = jnp.where(mask, q_ref[:, first:last], jnp.bfloat16(0))
        scores = []
        for (key, _), bias in zip(blocks, biases):
            product = lax.dot_general(
                query, key[:, first:last], NT, preferred_element_type=jnp.float32
            )
            scores.append(product * scale + bias)
        top = row_max(scores)
        total, mixed = 0.0, 0.0
        for score, (_, value) in zip(scores, blocks):
            weight = jnp.exp2(score - top)
            total = total + jnp.sum(weight, axis=1, keepdims=True)
            mixed = mixed + jnp.dot(
                weight.astype(jnp.bfloat16),
                value[:, first:last],
                preferred_element_type=jnp.float32,
            )
        mixed = jnp.where(mask, mixed, 0.0)
        max_ref[:, head : head + 1] = top
        sum_ref[:, head : head + 1] = total
        for at in range(first, last, LANES):
            part = mixed[:, at - first : at - first + LANES]
            if at < done:
                acc_ref[:, at : at + LANES] += part
            else:
                acc_ref[:, at : at + LANES] = part
                done = at + LANES


def layout_attention(band, counts, queries, blocks):
    tokens, width = queries.shape
    rows = tokens // CHUNKS
    slots = blocks[0].shape[0]
    smem = pl.BlockSpec(memory_space=pltpu.SMEM)
    row = pl.BlockSpec((rows, width), lambda i: (i, 0))
    stat = pl.BlockSpec((rows, LANES), lambda i: (i, 0))
    operands, specs = [], []
    for block in blocks:
        operands += [block, block]
        specs += [
            pl.BlockSpec((slots, width), lambda i: (0, 0)),
            pl.BlockSpec((slots, width), lambda i: (0, 1)),
        ]
    return pl.pallas_call(
        layout_kernel,
        grid=(CHUNKS,),
        in_specs=[smem, smem, row] + specs,
        out_specs=[row, stat, stat],
        out_shape=[
            jax.ShapeDtypeStruct((tokens, width), jnp.float32),
            jax.ShapeDtypeStruct((tokens, LANES), jnp.float32),
            jax.ShapeDtypeStruct((tokens, LANES), jnp.float32),
        ],
        compiler_params=pltpu.CompilerParams(vmem_limit_bytes=VMEM_LIMIT),
        name="layout_attention",
    )(band, counts, queries, *operands)


def view_kernel(
    half, shared_ref, q_ref, hidden_ref, acc_ref, max_ref, sum_ref,
    left_key, left_value, right_key, right_value, out_ref, mixed_ref,
):
    rows, width = q_ref.shape
    scale = LOG2E / math.sqrt(width // HEADS)
    count = left_key.shape[0]
    column = lax.rem(lane_index(count), half)
    left_bias = jnp.where(column >= half - shared_ref[0, 0], 0.0, DEAD)
    right_bias = jnp.where(column < shared_ref[0, 1], 0.0, DEAD)
    done = 0
    for head in range(HEADS):
        low, high, first, last = head_span(head, width)
        mask = head_mask(head, rows, width)
        query = jnp.where(mask, q_ref[:, first:last], jnp.bfloat16(0))
        scores = []
        for key, bias in ((left_key, left_bias), (right_key, right_bias)):
            product = lax.dot_general(
                query, key[:, first:last], NT, preferred_element_type=jnp.float32
            )
            scores.append(product * scale + bias)
        before = max_ref[:, head : head + 1]
        top = jnp.maximum(row_max(scores), before)
        carry = jnp.exp2(before - top)
        total = sum_ref[:, head : head + 1] * carry
        mixed = acc_ref[:, first:last] * carry
        for score, value in zip(scores, (left_value, right_value)):
            weight = jnp.exp2(score - top)
            total = total + jnp.sum(weight, axis=1, keepdims=True)
            mixed = mixed + jnp.dot(
                weight.astype(jnp.bfloat16),
                value[:, first:last],
                preferred_element_type=jnp.float32,
            )
        mixed = jnp.where(mask, mixed * (1.0 / total), 0.0)
        for at in range(first, last, LANES):
            part = mixed[:, at - first : at - first + LANES]
            if at < done:
                mixed_ref[:, at : at + LANES] += part
            else:
                mixed_ref[:, at : at + LANES] = part
                done = at + LANES
    out_ref[...] = (hidden_ref[...].astype(jnp.float32) + mixed_ref[...]).astype(jnp.bfloat16)


def view_attention(chunk, half, shared, queries, hidden, partial, left, right):
    tokens, width = queries.shape
    rows = tokens // CHUNKS
    keys = left.shape[0]
    row = pl.BlockSpec((rows, width), lambda i: (chunk, 0))
    stat = pl.BlockSpec((rows, LANES), lambda i: (chunk, 0))
    key_spec = pl.BlockSpec((keys, width), lambda i: (0, 0))
    value_spec = pl.BlockSpec((keys, width), lambda i: (0, 1))
    return pl.pallas_call(
        functools.partial(view_kernel, half),
        grid=(1,),
        in_specs=[
            pl.BlockSpec(memory_space=pltpu.SMEM), row, row, row, stat, stat,
            key_spec, value_spec, key_spec, value_spec,
        ],
        out_specs=pl.BlockSpec((rows, width), lambda i: (0, 0)),
        out_shape=jax.ShapeDtypeStruct((rows, width), jnp.bfloat16),
        scratch_shapes=[pltpu.VMEM((rows, width), jnp.float32)],
        compiler_params=pltpu.CompilerParams(vmem_limit_bytes=VMEM_LIMIT),
        name="view_attention",
    )(shared, queries, hidden, *partial, left, left, right, right)


def temporal_kernel(x_ref, gain_ref, w_ref, out_ref, normed_ref, qkv_ref):
    frames, group, width = x_ref.shape
    rows = frames * group
    scale = LOG2E / math.sqrt(width // HEADS)
    state = x_ref[...].reshape(rows, width).astype(jnp.float32)
    inverse = lax.rsqrt(jnp.mean(state * state, axis=1, keepdims=True) + EPSILON)
    normed_ref[...] = (state * inverse * gain_ref[...]).astype(jnp.bfloat16)
    step = 3 * LANES
    for at in range(0, 3 * width, step):
        qkv_ref[:, at : at + step] = jnp.dot(
            normed_ref[...], w_ref[:, at : at + step], preferred_element_type=jnp.float32
        ).astype(jnp.bfloat16)
    row = lax.broadcasted_iota(jnp.int32, (rows, rows), 0)
    column = lax.broadcasted_iota(jnp.int32, (rows, rows), 1)
    bias = jnp.where(lax.rem(row, group) == lax.rem(column, group), 0.0, DEAD)
    tiles = {}
    for head in range(HEADS):
        low, high, first, last = head_span(head, width)
        mask = head_mask(head, rows, width)
        query = jnp.where(mask, qkv_ref[:, first:last], jnp.bfloat16(0))
        key = qkv_ref[:, width + first : width + last]
        value = qkv_ref[:, 2 * width + first : 2 * width + last]
        score = lax.dot_general(query, key, NT, preferred_element_type=jnp.float32)
        score = score * scale + bias
        weight = jnp.exp2(score - jnp.max(score, axis=1, keepdims=True))
        total = jnp.sum(weight, axis=1, keepdims=True)
        mixed = jnp.dot(weight.astype(jnp.bfloat16), value, preferred_element_type=jnp.float32)
        mixed = jnp.where(mask, mixed * (1.0 / total), 0.0)
        for at in range(first, last, LANES):
            part = mixed[:, at - first : at - first + LANES]
            tiles[at] = tiles[at] + part if at in tiles else part
            if high >= at + LANES:
                out_ref[:, :, at : at + LANES] = (
                    tiles.pop(at).astype(jnp.bfloat16).reshape(frames, group, LANES)
                )


def temporal_attention(regrouped, norm_gain, w_qkv):
    frames, group, width = regrouped.shape
    rows = frames * group
    return pl.pallas_call(
        temporal_kernel,
        out_shape=jax.ShapeDtypeStruct(regrouped.shape, jnp.bfloat16),
        scratch_shapes=[
            pltpu.VMEM((rows, width), jnp.bfloat16),
            pltpu.VMEM((rows, 3 * width), jnp.bfloat16),
        ],
        compiler_params=pltpu.CompilerParams(vmem_limit_bytes=VMEM_LIMIT),
        name="temporal_attention",
    )(regrouped, norm_gain.reshape(1, width), w_qkv)


def exchange(array, axis, flip):
    length = lax.axis_size(axis)
    return lax.ppermute(array, axis, [(i, i ^ flip) for i in range(length)])


def passed_along(array, axis, by):
    length = lax.axis_size(axis)
    return lax.ppermute(array, axis, [(i, (i + by) % length) for i in range(length)])


def regroup(array):
    return lax.all_to_all(array, "frame", split_axis=0, concat_axis=0, tiled=True)


def per_device(
    hidden, cond_queries, cond_kv, layout_kv, layout_count, intersection, norm_gain, w_qkv
):
    patch_rows, patch_cols, width = hidden.shape[2:]
    half = patch_cols // 2
    tokens = patch_rows * patch_cols
    frames = lax.axis_size("frame")
    own = cond_kv[0, 0]
    left = passed_along(own[:, half:, :], "view", 1).reshape(patch_rows * half, 2 * width)
    right = passed_along(own[:, :half, :], "view", -1).reshape(patch_rows * half, 2 * width)
    layout = layout_kv[0]
    across = exchange(layout, "band", 2)
    beside = exchange(layout, "band", 1)
    diagonal = exchange(across, "band", 1)
    band = lax.axis_index("band").reshape(1)
    queries = cond_queries[0, 0].reshape(tokens, width)
    hidden_rows = hidden[0, 0].reshape(tokens, width)
    partial = layout_attention(
        band, layout_count, queries, [layout, beside, across, diagonal]
    )
    outputs = []
    for chunk in range(CHUNKS):
        state = view_attention(
            chunk, half, intersection, queries, hidden_rows, partial, left, right
        )
        regrouped = regroup(state.reshape(frames, -1, width))
        outputs.append(regroup(temporal_attention(regrouped, norm_gain, w_qkv)))
    rows = [output.reshape(tokens // CHUNKS, width) for output in outputs]
    return jnp.concatenate(rows, axis=0).reshape(1, 1, patch_rows, patch_cols, width)


def solution(mesh):
    in_specs = (
        P("view", "frame", "band", None, None),
        P("view", "frame", "band", None, None),
        P("view", "frame", "band", None, None),
        P("frame", "band", None),
        P("frame", None),
        P("view", None),
        P(),
        P(),
    )
    out_specs = P("view", "frame", "band", None, None)
    return jax.shard_map(
        per_device, mesh=mesh, in_specs=in_specs, out_specs=out_specs, check_vma=False
    )
```

```python
import functools
import math

import jax
import jax.numpy as jnp
from jax import lax
from jax.experimental import pallas as pl
from jax.experimental.pallas import tpu as pltpu
from jax.sharding import PartitionSpec as P

HEADS = 16
LANES = 128
HEAD_STEPS = (0, 6, 11, 16)
QUERY_ROWS = 256
EPSILON = 1e-06
DEAD = -1e30
VMEM_LIMIT = 32 << 20
LOG2E = 1.4426950408889634
NT = (((1,), (1,)), ((), ()))


def head_span(head, width):
    size = width // HEADS
    low, high = head * size, (head + 1) * size
    return low, high, low // LANES * LANES, -(-high // LANES) * LANES


def head_mask(head, rows, width):
    low, high, first, last = head_span(head, width)
    column = lax.broadcasted_iota(jnp.int32, (rows, last - first), 1) + first
    return (column >= low) & (column < high)


def lane_index(count):
    return lax.broadcasted_iota(jnp.int32, (1, count), 1)


def over_lanes(reduce_lanes, combine, pieces):
    tiles = [
        piece[:, at : at + LANES] for piece in pieces for at in range(0, piece.shape[1], LANES)
    ]
    while len(tiles) > 1:
        pairs = [combine(a, b) for a, b in zip(tiles[0::2], tiles[1::2])]
        tiles = pairs + tiles[len(tiles) // 2 * 2 :]
    return reduce_lanes(tiles[0], axis=1, keepdims=True)


def column_cuts(width):
    return (0, *(head_span(end - 1, width)[3] for end in HEAD_STEPS[1:]))


def cond_kernel(half, width, heads, cuts, count_kv, *refs):
    count_ref, shared_ref, q_ref, hidden_ref = refs[:4]
    layout_refs = refs[4:8]
    kv_refs = refs[8 : 8 + 2 * count_kv]
    rest = list(refs[8 + 2 * count_kv :])
    mixed_ref, key_ref, value_ref, sems = rest[-4:]
    last_step = heads[1] == HEADS
    finished = []
    if last_step:
        finished, rest = rest[: count_kv - 1], rest[count_kv - 1 :]
    carry_ref = rest.pop(0) if heads[0] > 0 else None
    out_ref = rest[0]
    rows = q_ref.shape[0]
    scale = LOG2E / math.sqrt(width // HEADS)
    begin = head_span(heads[0], width)[2]
    finish = head_span(heads[1] - 1, width)[3]
    keys = kv_refs[0].shape[0]
    slots = layout_refs[0].shape[0]

    @pl.when(pl.program_id(0) == 0)
    def _():
        moves = []
        for part in range(count_kv):
            start, end = max(cuts[part], begin), min(cuts[part + 1], finish)
            size = cuts[part + 1] - cuts[part]
            for side in range(2 if start < end else 0):
                low = start - cuts[part]
                moves.append((kv_refs[2 * part + side], low, size + low, side * keys, start, end))
        for block, ref in enumerate(layout_refs):
            at = 2 * keys + block * slots
            moves.append((ref, begin, width + begin, at, begin, finish))
        copies = []
        for which, target in enumerate((key_ref, value_ref)):
            for move in moves:
                ref, at, start, end = move[0], move[3], move[4], move[5]
                low = move[1 + which]
                copies.append(
                    pltpu.make_async_copy(
                        ref.at[:, low : low + end - start],
                        target.at[at : at + ref.shape[0], start - begin : end - begin],
                        sems.at[len(copies)],
                    )
                )
        for copy in copies:
            copy.start()
        for copy in copies:
            copy.wait()

    band = lax.axis_index("band")
    column = lax.rem(lane_index(keys), half)
    live = [column >= half - shared_ref[0, 0], column < shared_ref[0, 1]]
    for block in range(len(layout_refs)):
        limit = count_ref[0, jnp.bitwise_xor(band, block)]
        live.append(lane_index(slots) < limit)
    bias = jnp.concatenate([jnp.where(mask, 0.0, DEAD) for mask in live], axis=1)

    def scores_of(head):
        low, high, first, last = head_span(head, width)
        query = jnp.where(head_mask(head, rows, width), q_ref[:, first:last], jnp.bfloat16(0))
        product = lax.dot_general(
            query, key_ref[:, first - begin : last - begin], NT,
            preferred_element_type=jnp.float32,
        )
        return product * scale + bias

    done = begin
    if carry_ref is not None:
        mixed_ref[:, 0:LANES] = carry_ref[...]
        done = begin + LANES
    scores = scores_of(heads[0])
    for head in range(*heads):
        following = scores_of(head + 1) if head + 1 < heads[1] else None
        low, high, first, last = head_span(head, width)
        weights = jnp.exp2(scores - over_lanes(jnp.max, jnp.maximum, [scores]))
        total = over_lanes(jnp.sum, jnp.add, [weights])
        mixed = jnp.dot(
            weights.astype(jnp.bfloat16), value_ref[:, first - begin : last - begin],
            preferred_element_type=jnp.float32,
        )
        mixed = jnp.where(head_mask(head, rows, width), mixed * (1.0 / total), 0.0)
        for at in range(first, last, LANES):
            part = mixed[:, at - first : at - first + LANES]
            if at < done:
                mixed_ref[:, at - begin : at - begin + LANES] += part
            else:
                mixed_ref[:, at - begin : at - begin + LANES] = part
                done = at + LANES
        scores = following
    at = 0
    for ref in finished:
        out_ref[:, at : at + ref.shape[1]] = ref[...]
        at += ref.shape[1]
    size = out_ref.shape[1] - at
    out_ref[:, at:] = (
        hidden_ref[:, begin : begin + size].astype(jnp.float32) + mixed_ref[:, :size]
    ).astype(jnp.bfloat16)
    if not last_step:
        rest[1][...] = mixed_ref[:, size : size + LANES]


def cond_attention(half, step, scalars, queries, hidden, layout, kv_parts, finished, carry):
    tokens, width = queries.shape
    heads = HEAD_STEPS[step], HEAD_STEPS[step + 1]
    cuts = column_cuts(width)
    last_step = heads[1] == HEADS
    begin = head_span(heads[0], width)[2]
    read = head_span(heads[1] - 1, width)[3]
    size = width if last_step else heads[1] * (width // HEADS) // LANES * LANES - begin
    smem = pl.BlockSpec(memory_space=pltpu.SMEM)

    def rows_of(columns):
        return pl.BlockSpec((QUERY_ROWS, columns), lambda i: (i, 0))

    flat = [array for pair in kv_parts for array in pair]
    operands = [*scalars, queries, hidden, *layout, *flat]
    specs = [smem, smem, rows_of(read), rows_of(read)]
    specs += [pl.BlockSpec(memory_space=pltpu.VMEM) for _ in (*layout, *flat)]
    keys = 2 * flat[0].shape[0] + len(layout) * layout[0].shape[0]
    copies = 2 * (len(layout) + len(flat))
    if last_step:
        operands += finished
        specs += [rows_of(array.shape[1]) for array in finished]
    if carry is not None:
        operands.append(carry)
        specs.append(rows_of(LANES))
    out_specs = [rows_of(size)]
    out_shape = [jax.ShapeDtypeStruct((tokens, size), jnp.bfloat16)]
    if last_step:
        out_shape = [pltpu.HBM((tokens, size), jnp.bfloat16)]
    else:
        out_specs.append(rows_of(LANES))
        out_shape.append(jax.ShapeDtypeStruct((tokens, LANES), jnp.float32))
    return pl.pallas_call(
        functools.partial(cond_kernel, half, width, heads, cuts, len(kv_parts)),
        grid=(tokens // QUERY_ROWS,),
        in_specs=specs,
        out_specs=out_specs,
        out_shape=out_shape,
        scratch_shapes=[
            pltpu.VMEM((QUERY_ROWS, read - begin), jnp.float32),
            pltpu.VMEM((keys, read - begin), jnp.bfloat16),
            pltpu.VMEM((keys, read - begin), jnp.bfloat16),
            pltpu.SemaphoreType.DMA((copies,)),
        ],
        compiler_params=pltpu.CompilerParams(vmem_limit_bytes=VMEM_LIMIT),
        name="cond_attention",
    )(*operands)


def temporal_kernel(
    x_ref, gain_ref, w_ref, out_ref, normed_ref, qkv_ref
):
    frames, positions, width = out_ref.shape
    group = 16
    rows = frames * group
    scale = LOG2E / math.sqrt(width // HEADS)
    step = pl.program_id(0)

    @pl.when(step == 0)
    def _():
        for at in range(0, positions, group):
            state = x_ref[:, at : at + group, :].reshape(rows, width).astype(jnp.float32)
            inverse = lax.rsqrt(jnp.mean(state * state, axis=1, keepdims=True) + EPSILON)
            normed_ref[at * frames : at * frames + rows, :] = (
                state * inverse * gain_ref[...]
            ).astype(jnp.bfloat16)

    for part in range(3):

        @pl.when(step == part)
        def _():
            qkv_ref[:, part * width : (part + 1) * width] = jnp.dot(
                normed_ref[...], w_ref[...], preferred_element_type=jnp.float32
            ).astype(jnp.bfloat16)

    @pl.when(step == 2)
    def _():
        row = lax.broadcasted_iota(jnp.int32, (rows, rows), 0)
        column = lax.broadcasted_iota(jnp.int32, (rows, rows), 1)
        bias = jnp.where(lax.rem(row, group) == lax.rem(column, group), 0.0, DEAD)
        for at in range(0, positions, group):
            span = slice(at * frames, at * frames + rows)
            tiles = {}
            for head in range(HEADS):
                low, high, first, last = head_span(head, width)
                mask = head_mask(head, rows, width)
                query = jnp.where(mask, qkv_ref[span, first:last], jnp.bfloat16(0))
                key = qkv_ref[span, width + first : width + last]
                value = qkv_ref[span, 2 * width + first : 2 * width + last]
                score = lax.dot_general(query, key, NT, preferred_element_type=jnp.float32)
                score = score * scale + bias
                weight = jnp.exp2(score - over_lanes(jnp.max, jnp.maximum, [score]))
                total = over_lanes(jnp.sum, jnp.add, [weight])
                mixed = jnp.dot(
                    weight.astype(jnp.bfloat16), value, preferred_element_type=jnp.float32
                )
                mixed = jnp.where(mask, mixed * (1.0 / total), 0.0)
                for tile in range(first, last, LANES):
                    part = mixed[:, tile - first : tile - first + LANES]
                    tiles[tile] = tiles[tile] + part if tile in tiles else part
                    if high >= tile + LANES:
                        out_ref[:, at : at + group, tile : tile + LANES] = (
                            tiles.pop(tile).astype(jnp.bfloat16).reshape(frames, group, LANES)
                        )


def temporal_attention(regrouped, norm_gain, w_qkv):
    frames, positions, width = regrouped.shape
    whole = pl.BlockSpec(regrouped.shape, lambda i: (0, 0, 0))
    return pl.pallas_call(
        temporal_kernel,
        grid=(3,),
        in_specs=[
            whole,
            pl.BlockSpec((1, width), lambda i: (0, 0)),
            pl.BlockSpec((width, width), lambda i: (0, i)),
        ],
        out_specs=whole,
        out_shape=jax.ShapeDtypeStruct((frames, positions, width), jnp.bfloat16),
        scratch_shapes=[
            pltpu.VMEM((frames * positions, width), jnp.bfloat16),
            pltpu.VMEM((frames * positions, 3 * width), jnp.bfloat16),
        ],
        compiler_params=pltpu.CompilerParams(vmem_limit_bytes=VMEM_LIMIT),
        name="temporal_attention",
    )(
        regrouped,
        norm_gain.reshape(1, width),
        pltpu.with_memory_space_constraint(w_qkv, pltpu.HBM),
    )


def split_kernel(half, cuts, kv_ref, *refs):
    out_refs, sems = refs[:-1], refs[-1]
    width = kv_ref.shape[2] // 2
    copies = []
    for piece, (start, end) in enumerate(zip(cuts, cuts[1:])):
        size = end - start
        for side, columns in enumerate((slice(half, 2 * half), slice(0, half))):
            out_ref = out_refs[2 * piece + side]
            for part in range(2):
                low = part * width + start
                copies.append(
                    pltpu.make_async_copy(
                        kv_ref.at[:, columns, low : low + size],
                        out_ref.at[:, :, part * size : (part + 1) * size],
                        sems.at[len(copies)],
                    )
                )
    for copy in copies:
        copy.start()
    for copy in copies:
        copy.wait()


def split_halves(own, cuts):
    rows, columns = own.shape[:2]
    shapes = [
        jax.ShapeDtypeStruct((rows, columns // 2, 2 * (end - start)), own.dtype)
        for start, end in zip(cuts, cuts[1:])
        for _ in range(2)
    ]
    local = pl.BlockSpec(memory_space=pltpu.VMEM)
    pieces = pl.pallas_call(
        functools.partial(split_kernel, columns // 2, cuts),
        in_specs=[pl.BlockSpec(memory_space=pltpu.HBM)],
        out_specs=[local] * len(shapes),
        out_shape=shapes,
        scratch_shapes=[pltpu.SemaphoreType.DMA((2 * len(shapes),))],
        compiler_params=pltpu.CompilerParams(vmem_limit_bytes=VMEM_LIMIT),
        name="split_halves",
    )(own)
    return list(zip(pieces[0::2], pieces[1::2]))


def exchange(array, axis, flip):
    length = lax.axis_size(axis)
    return lax.ppermute(array, axis, [(i, i ^ flip) for i in range(length)])


def passed_along(array, axis, by):
    length = lax.axis_size(axis)
    return lax.ppermute(array, axis, [(i, (i + by) % length) for i in range(length)])


def regroup(array):
    return lax.all_to_all(array, "frame", split_axis=0, concat_axis=0, tiled=True)


def per_device(
    hidden, cond_queries, cond_kv, layout_kv, layout_count, intersection, norm_gain, w_qkv
):
    patch_rows, patch_cols, width = hidden.shape[2:]
    half = patch_cols // 2
    tokens = patch_rows * patch_cols
    frames = lax.axis_size("frame")
    cuts = column_cuts(width)
    own = cond_kv[0, 0]

    def sent(pair):
        return tuple(
            passed_along(side, "view", by).reshape(patch_rows * half, -1)
            for side, by in zip(pair, (1, -1))
        )

    layout = layout_kv[0]
    (first_source,) = split_halves(own, cuts[:2])
    first = sent(first_source)
    across = exchange(layout, "band", 2)
    beside = exchange(layout, "band", 1)
    sources, across = lax.optimization_barrier((split_halves(own, cuts[1:]), across))
    diagonal = exchange(across, "band", 1)
    second = sent(sources[0])
    last_source, first = lax.optimization_barrier((sources[1], first))
    kv_parts = [first, second, sent(last_source)]
    layout = (layout, beside, across, diagonal)
    scalars = (layout_count, intersection)
    queries = cond_queries[0, 0].reshape(tokens, width)
    hidden_rows = hidden[0, 0].reshape(tokens, width)
    finished, carry = [], None
    for step in range(len(kv_parts)):
        result = cond_attention(
            half, step, scalars, queries, hidden_rows, layout, kv_parts[: step + 1],
            finished, carry,
        )
        finished, carry = finished + [result[0]], result[-1]
    regrouped = regroup(finished[-1].reshape(frames, -1, width))
    output = regroup(temporal_attention(regrouped, norm_gain, w_qkv))
    return output.reshape(1, 1, patch_rows, patch_cols, width)


def solution(mesh):
    in_specs = (
        P("view", "frame", "band", None, None),
        P("view", "frame", "band", None, None),
        P("view", "frame", "band", None, None),
        P("frame", "band", None),
        P("frame", None),
        P("view", None),
        P(),
        P(),
    )
    out_specs = P("view", "frame", "band", None, None)
    return jax.shard_map(
        per_device, mesh=mesh, in_specs=in_specs, out_specs=out_specs, check_vma=False
    )
```

```python
import functools
import math

import jax
import jax.numpy as jnp
from jax import lax
from jax.experimental import pallas as pl
from jax.experimental.pallas import tpu as pltpu
from jax.sharding import PartitionSpec as P

HEADS = 16
LANES = 128
HEAD_STEPS = (0, 7, 12, 16)
QUERY_ROWS = 512
EPSILON = 1e-06
DEAD = -1e30
VMEM_LIMIT = 32 << 20
LIVE_LAYOUT = 320
ALIGN = 16
LOG2E = 1.4426950408889634
NT = (((1,), (1,)), ((), ()))


def head_span(head, width):
    size = width // HEADS
    low, high = head * size, (head + 1) * size
    return low, high, low // LANES * LANES, -(-high // LANES) * LANES


def head_mask(head, rows, width):
    low, high, first, last = head_span(head, width)
    column = lax.broadcasted_iota(jnp.int32, (rows, last - first), 1) + first
    return (column >= low) & (column < high)


def lane_index(count):
    return lax.broadcasted_iota(jnp.int32, (1, count), 1)


def over_lanes(reduce_lanes, combine, pieces):
    tiles = [
        piece[:, at : at + LANES] for piece in pieces for at in range(0, piece.shape[1], LANES)
    ]
    while len(tiles) > 1:
        pairs = [combine(a, b) for a, b in zip(tiles[0::2], tiles[1::2])]
        tiles = pairs + tiles[len(tiles) // 2 * 2 :]
    return reduce_lanes(tiles[0], axis=1, keepdims=True)


def column_cuts(width):
    return (0, *(head_span(end - 1, width)[3] for end in HEAD_STEPS[1:]))


def cond_kernel(half, width, heads, cuts, count_kv, *refs):
    count_ref, shared_ref, q_ref, hidden_ref = refs[:4]
    layout_refs = refs[4:8]
    kv_refs = refs[8 : 8 + 2 * count_kv]
    rest = list(refs[8 + 2 * count_kv :])
    mixed_ref, key_ref, value_ref = rest[-3:]
    last_step = heads[1] == HEADS
    finished = []
    if last_step:
        finished, rest = rest[: count_kv - 1], rest[count_kv - 1 :]
    carry_ref = rest.pop(0) if heads[0] > 0 else None
    out_ref = rest[0]
    rows = q_ref.shape[0]
    scale = LOG2E / math.sqrt(width // HEADS)
    begin = head_span(heads[0], width)[2]
    finish = head_span(heads[1] - 1, width)[3]
    keys = kv_refs[0].shape[0]
    slots = layout_refs[0].shape[0]

    band = lax.axis_index("band")
    limits = [count_ref[0, jnp.bitwise_xor(band, block)] for block in range(len(layout_refs))]
    offsets = [2 * keys]
    for limit in limits:
        offsets.append(offsets[-1] + (limit + ALIGN - 1) // ALIGN * ALIGN)

    @pl.when(pl.program_id(0) == 0)
    def _():
        for target, shift in ((key_ref, 0), (value_ref, 1)):
            for part in range(count_kv):
                start, end = max(cuts[part], begin), min(cuts[part + 1], finish)
                size = cuts[part + 1] - cuts[part]
                low = start - cuts[part] + shift * size
                for side in range(2 if start < end else 0):
                    target[side * keys : (side + 1) * keys, start - begin : end - begin] = (
                        kv_refs[2 * part + side][:, low : low + end - start]
                    )
            low = shift * width + begin
            spare = key_ref.shape[0] - slots
            columns = slice(low, low + finish - begin)
            for at in range(2 * keys, spare, slots):
                target[at : at + slots, :] = layout_refs[0][:, columns]
            for ref, offset in zip(layout_refs, offsets):
                at = pl.multiple_of(offset, ALIGN)
                target[pl.ds(at, slots), :] = ref[:, columns]

    used = key_ref.shape[0] - slots
    column = lax.rem(lane_index(keys), half)
    slot = lane_index(used - 2 * keys) + 2 * keys
    layout_live = slot < 0
    for limit, offset in zip(limits, offsets):
        layout_live |= (slot >= offset) & (slot < offset + limit)
    live = jnp.concatenate(
        [
            part.astype(jnp.int32)
            for part in (
                column >= half - shared_ref[0, 0], column < shared_ref[0, 1], layout_live
            )
        ],
        axis=1,
    ) > 0

    def scores_of(head):
        low, high, first, last = head_span(head, width)
        query = jnp.where(head_mask(head, rows, width), q_ref[:, first:last], jnp.bfloat16(0))
        product = lax.dot_general(
            query, key_ref[:used, first - begin : last - begin], NT,
            preferred_element_type=jnp.float32,
        )
        return jnp.where(live, product * scale, DEAD)

    done = begin
    if carry_ref is not None:
        mixed_ref[:, 0:LANES] = carry_ref[...]
        done = begin + LANES
    scores = scores_of(heads[0])
    for head in range(*heads):
        following = scores_of(head + 1) if head + 1 < heads[1] else None
        low, high, first, last = head_span(head, width)
        weights = jnp.exp2(scores - over_lanes(jnp.max, jnp.maximum, [scores]))
        total = over_lanes(jnp.sum, jnp.add, [weights])
        mixed = jnp.dot(
            weights.astype(jnp.bfloat16), value_ref[:used, first - begin : last - begin],
            preferred_element_type=jnp.float32,
        )
        mixed = jnp.where(head_mask(head, rows, width), mixed * (1.0 / total), 0.0)
        for at in range(first, last, LANES):
            part = mixed[:, at - first : at - first + LANES]
            if at < done:
                mixed_ref[:, at - begin : at - begin + LANES] += part
            else:
                mixed_ref[:, at - begin : at - begin + LANES] = part
                done = at + LANES
        scores = following
    at = 0
    for ref in finished:
        out_ref[:, at : at + ref.shape[1]] = ref[...]
        at += ref.shape[1]
    size = out_ref.shape[1] - at
    out_ref[:, at:] = (
        hidden_ref[:, begin : begin + size].astype(jnp.float32) + mixed_ref[:, :size]
    ).astype(jnp.bfloat16)
    if not last_step:
        rest[1][...] = mixed_ref[:, size : size + LANES]


def cond_attention(half, step, scalars, queries, hidden, layout, kv_parts, finished, carry):
    tokens, width = queries.shape
    heads = HEAD_STEPS[step], HEAD_STEPS[step + 1]
    cuts = column_cuts(width)
    last_step = heads[1] == HEADS
    begin = head_span(heads[0], width)[2]
    read = head_span(heads[1] - 1, width)[3]
    size = width if last_step else heads[1] * (width // HEADS) // LANES * LANES - begin
    smem = pl.BlockSpec(memory_space=pltpu.SMEM)

    def rows_of(columns):
        return pl.BlockSpec((QUERY_ROWS, columns), lambda i: (i, 0))

    flat = [array for pair in kv_parts for array in pair]
    operands = [*scalars, queries, hidden, *layout, *flat]
    specs = [smem, smem, rows_of(read), rows_of(read)]
    specs += [pl.BlockSpec(memory_space=pltpu.VMEM) for _ in (*layout, *flat)]
    slots = layout[0].shape[0]
    padded = LIVE_LAYOUT + (ALIGN - 1) * len(layout)
    keys = 2 * flat[0].shape[0] + -(-padded // slots) * slots + slots
    if last_step:
        operands += finished
        specs += [rows_of(array.shape[1]) for array in finished]
    if carry is not None:
        operands.append(carry)
        specs.append(rows_of(LANES))
    out_specs = [rows_of(size)]
    out_shape = [jax.ShapeDtypeStruct((tokens, size), jnp.bfloat16)]
    if last_step:
        out_shape = [pltpu.HBM((tokens, size), jnp.bfloat16)]
    else:
        out_specs.append(rows_of(LANES))
        out_shape.append(jax.ShapeDtypeStruct((tokens, LANES), jnp.float32))
    return pl.pallas_call(
        functools.partial(cond_kernel, half, width, heads, cuts, len(kv_parts)),
        grid=(tokens // QUERY_ROWS,),
        in_specs=specs,
        out_specs=out_specs,
        out_shape=out_shape,
        scratch_shapes=[
            pltpu.VMEM((QUERY_ROWS, read - begin), jnp.float32),
            pltpu.VMEM((keys, read - begin), jnp.bfloat16),
            pltpu.VMEM((keys, read - begin), jnp.bfloat16),
        ],
        compiler_params=pltpu.CompilerParams(vmem_limit_bytes=VMEM_LIMIT),
        name="cond_attention",
    )(*operands)


def temporal_kernel(
    x_ref, gain_ref, w_ref, out_ref, normed_ref, qkv_ref
):
    frames, positions, width = out_ref.shape
    group = 16
    rows = frames * group
    scale = LOG2E / math.sqrt(width // HEADS)
    step = pl.program_id(0)

    @pl.when(step == 0)
    def _():
        for at in range(0, positions, group):
            state = x_ref[:, at : at + group, :].reshape(rows, width).astype(jnp.float32)
            inverse = lax.rsqrt(jnp.mean(state * state, axis=1, keepdims=True) + EPSILON)
            normed_ref[at * frames : at * frames + rows, :] = (
                state * inverse * gain_ref[...]
            ).astype(jnp.bfloat16)

    for part in range(3):

        @pl.when(step == part)
        def _():
            qkv_ref[:, part * width : (part + 1) * width] = jnp.dot(
                normed_ref[...], w_ref[...], preferred_element_type=jnp.float32
            ).astype(jnp.bfloat16)

    @pl.when(step == 2)
    def _():
        row = lax.broadcasted_iota(jnp.int32, (rows, rows), 0)
        column = lax.broadcasted_iota(jnp.int32, (rows, rows), 1)
        same = lax.rem(row, group) == lax.rem(column, group)

        def scores_of(at, head):
            low, high, first, last = head_span(head, width)
            span = slice(at * frames, at * frames + rows)
            query = jnp.where(
                head_mask(head, rows, width), qkv_ref[span, first:last], jnp.bfloat16(0)
            )
            key = qkv_ref[span, width + first : width + last]
            score = lax.dot_general(query, key, NT, preferred_element_type=jnp.float32)
            return jnp.where(same, score * scale, DEAD)

        turns = [(at, head) for at in range(0, positions, group) for head in range(HEADS)]
        tiles = {}
        score = scores_of(*turns[0])
        for turn, (at, head) in enumerate(turns):
            following = scores_of(*turns[turn + 1]) if turn + 1 < len(turns) else None
            low, high, first, last = head_span(head, width)
            span = slice(at * frames, at * frames + rows)
            weight = jnp.exp2(score - over_lanes(jnp.max, jnp.maximum, [score]))
            total = over_lanes(jnp.sum, jnp.add, [weight])
            mixed = jnp.dot(
                weight.astype(jnp.bfloat16),
                qkv_ref[span, 2 * width + first : 2 * width + last],
                preferred_element_type=jnp.float32,
            )
            mixed = jnp.where(head_mask(head, rows, width), mixed * (1.0 / total), 0.0)
            for tile in range(first, last, LANES):
                part = mixed[:, tile - first : tile - first + LANES]
                tiles[tile] = tiles[tile] + part if tile in tiles else part
                if high >= tile + LANES:
                    out_ref[:, at : at + group, tile : tile + LANES] = (
                        tiles.pop(tile).astype(jnp.bfloat16).reshape(frames, group, LANES)
                    )
            score = following


def temporal_attention(regrouped, norm_gain, w_qkv):
    frames, positions, width = regrouped.shape
    whole = pl.BlockSpec(regrouped.shape, lambda i: (0, 0, 0))
    return pl.pallas_call(
        temporal_kernel,
        grid=(3,),
        in_specs=[
            whole,
            pl.BlockSpec((1, width), lambda i: (0, 0)),
            pl.BlockSpec((width, width), lambda i: (0, i)),
        ],
        out_specs=whole,
        out_shape=jax.ShapeDtypeStruct((frames, positions, width), jnp.bfloat16),
        scratch_shapes=[
            pltpu.VMEM((frames * positions, width), jnp.bfloat16),
            pltpu.VMEM((frames * positions, 3 * width), jnp.bfloat16),
        ],
        compiler_params=pltpu.CompilerParams(vmem_limit_bytes=VMEM_LIMIT),
        name="temporal_attention",
    )(
        regrouped,
        norm_gain.reshape(1, width),
        pltpu.with_memory_space_constraint(w_qkv, pltpu.HBM),
    )


def split_kernel(half, cuts, kv_ref, *refs):
    out_refs, sems = refs[:-1], refs[-1]
    width = kv_ref.shape[2] // 2
    copies = []
    for piece, (start, end) in enumerate(zip(cuts, cuts[1:])):
        size = end - start
        for side, columns in enumerate((slice(half, 2 * half), slice(0, half))):
            out_ref = out_refs[2 * piece + side]
            for part in range(2):
                low = part * width + start
                copies.append(
                    pltpu.make_async_copy(
                        kv_ref.at[:, columns, low : low + size],
                        out_ref.at[:, :, part * size : (part + 1) * size],
                        sems.at[len(copies)],
                    )
                )
    for copy in copies:
        copy.start()
    for copy in copies:
        copy.wait()


def split_halves(own, cuts):
    rows, columns = own.shape[:2]
    shapes = [
        jax.ShapeDtypeStruct((rows, columns // 2, 2 * (end - start)), own.dtype)
        for start, end in zip(cuts, cuts[1:])
        for _ in range(2)
    ]
    local = pl.BlockSpec(memory_space=pltpu.VMEM)
    pieces = pl.pallas_call(
        functools.partial(split_kernel, columns // 2, cuts),
        in_specs=[pl.BlockSpec(memory_space=pltpu.HBM)],
        out_specs=[local] * len(shapes),
        out_shape=shapes,
        scratch_shapes=[pltpu.SemaphoreType.DMA((2 * len(shapes),))],
        compiler_params=pltpu.CompilerParams(vmem_limit_bytes=VMEM_LIMIT),
        name="split_halves",
    )(own)
    return list(zip(pieces[0::2], pieces[1::2]))


def exchange(array, axis, flip):
    length = lax.axis_size(axis)
    return lax.ppermute(array, axis, [(i, i ^ flip) for i in range(length)])


def passed_along(array, axis, by):
    length = lax.axis_size(axis)
    return lax.ppermute(array, axis, [(i, (i + by) % length) for i in range(length)])


def regroup(array):
    return lax.all_to_all(array, "frame", split_axis=0, concat_axis=0, tiled=True)


def per_device(
    hidden, cond_queries, cond_kv, layout_kv, layout_count, intersection, norm_gain, w_qkv
):
    patch_rows, patch_cols, width = hidden.shape[2:]
    half = patch_cols // 2
    tokens = patch_rows * patch_cols
    frames = lax.axis_size("frame")
    cuts = column_cuts(width)
    own = pltpu.with_memory_space_constraint(cond_kv[0, 0], pltpu.HBM)

    def sent(pair):
        return tuple(
            passed_along(side, "view", by).reshape(patch_rows * half, -1)
            for side, by in zip(pair, (1, -1))
        )

    layout = layout_kv[0]
    (first_source,) = split_halves(own, cuts[:2])
    first = sent(first_source)
    across = exchange(layout, "band", 2)
    beside = exchange(layout, "band", 1)
    sources, across = lax.optimization_barrier((split_halves(own, cuts[1:]), across))
    diagonal = exchange(across, "band", 1)
    second = sent(sources[0])
    last_source, first = lax.optimization_barrier((sources[1], first))
    kv_parts = [first, second, sent(last_source)]
    layout = (layout, beside, across, diagonal)
    scalars = (layout_count, intersection)
    queries = cond_queries[0, 0].reshape(tokens, width)
    hidden_rows = hidden[0, 0].reshape(tokens, width)
    finished, carry = [], None
    for step in range(len(kv_parts)):
        result = cond_attention(
            half, step, scalars, queries, hidden_rows, layout, kv_parts[: step + 1],
            finished, carry,
        )
        finished, carry = finished + [result[0]], result[-1]
    regrouped = regroup(finished[-1].reshape(frames, -1, width))
    output = regroup(temporal_attention(regrouped, norm_gain, w_qkv))
    return output.reshape(1, 1, patch_rows, patch_cols, width)


def solution(mesh):
    in_specs = (
        P("view", "frame", "band", None, None),
        P("view", "frame", "band", None, None),
        P("view", "frame", "band", None, None),
        P("frame", "band", None),
        P("frame", None),
        P("view", None),
        P(),
        P(),
    )
    out_specs = P("view", "frame", "band", None, None)
    return jax.shard_map(
        per_device, mesh=mesh, in_specs=in_specs, out_specs=out_specs, check_vma=False
    )
```

```python
import functools
import math

import jax
import jax.numpy as jnp
from jax import lax
from jax.experimental import pallas as pl
from jax.experimental.pallas import tpu as pltpu
from jax.sharding import PartitionSpec as P

HEADS = 16
LANES = 128
HEAD_STEPS = (0, 8, 12, 16)
EPSILON = 1e-06
DEAD = -1e30
VMEM_LIMIT = 32 << 20
LIVE_LAYOUT = 320
ALIGN = 16
LOG2E = 1.4426950408889634
NT = (((1,), (1,)), ((), ()))


def head_span(head, width):
    size = width // HEADS
    low, high = head * size, (head + 1) * size
    return low, high, low // LANES * LANES, -(-high // LANES) * LANES


def head_mask(head, rows, width):
    low, high, first, last = head_span(head, width)
    column = lax.broadcasted_iota(jnp.int32, (rows, last - first), 1) + first
    return (column >= low) & (column < high)


def lane_index(count):
    return lax.broadcasted_iota(jnp.int32, (1, count), 1)


def over_lanes(reduce_lanes, combine, pieces):
    tiles = [
        piece[:, at : at + LANES] for piece in pieces for at in range(0, piece.shape[1], LANES)
    ]
    while len(tiles) > 1:
        pairs = [combine(a, b) for a, b in zip(tiles[0::2], tiles[1::2])]
        tiles = pairs + tiles[len(tiles) // 2 * 2 :]
    return reduce_lanes(tiles[0], axis=1, keepdims=True)


def column_cuts(width):
    return (0, *(head_span(end - 1, width)[3] for end in HEAD_STEPS[1:]))


def cond_kernel(half, width, heads, cuts, count_kv, *refs):
    count_ref, shared_ref, q_ref, hidden_ref = refs[:4]
    layout_refs = refs[4:8]
    kv_refs = refs[8 : 8 + 2 * count_kv]
    rest = list(refs[8 + 2 * count_kv :])
    mixed_ref, key_ref, value_ref, state_ref, sems = rest[-5:]
    last_step = heads[1] == HEADS
    finished = []
    if last_step:
        finished, rest = rest[: count_kv - 1], rest[count_kv - 1 :]
    carry_ref = rest.pop(0) if heads[0] > 0 else None
    out_ref = rest[0]
    rows = q_ref.shape[0]
    scale = LOG2E / math.sqrt(width // HEADS)
    begin = head_span(heads[0], width)[2]
    finish = head_span(heads[1] - 1, width)[3]
    keys = kv_refs[0].shape[0]
    slots = layout_refs[0].shape[0]

    moves = []
    if last_step:
        at = 0
        for index, ref in enumerate((*finished, state_ref)):
            columns = slice(at, at + ref.shape[1])
            moves.append(pltpu.make_async_copy(ref, out_ref.at[:, columns], sems.at[index]))
            at += ref.shape[1]
        for move in moves[:-1]:
            move.start()

    band = lax.axis_index("band")
    limits = [count_ref[0, jnp.bitwise_xor(band, block)] for block in range(len(layout_refs))]
    offsets = [2 * keys]
    for limit in limits:
        offsets.append(offsets[-1] + (limit + ALIGN - 1) // ALIGN * ALIGN)

    for target, shift in ((key_ref, 0), (value_ref, 1)):
        for part in range(count_kv):
            start, end = max(cuts[part], begin), min(cuts[part + 1], finish)
            size = cuts[part + 1] - cuts[part]
            low = start - cuts[part] + shift * size
            for side in range(2 if start < end else 0):
                target[side * keys : (side + 1) * keys, start - begin : end - begin] = (
                    kv_refs[2 * part + side][:, low : low + end - start]
                )
        low = shift * width + begin
        spare = key_ref.shape[0] - slots
        columns = slice(low, low + finish - begin)
        for at in range(2 * keys, spare, slots):
            target[at : at + slots, :] = layout_refs[0][:, columns]
        for ref, offset in zip(layout_refs, offsets):
            at = pl.multiple_of(offset, ALIGN)
            target[pl.ds(at, slots), :] = ref[:, columns]

    used = key_ref.shape[0] - slots
    column = lax.rem(lane_index(keys), half)
    slot = lane_index(used - 2 * keys) + 2 * keys
    layout_live = slot < 0
    for limit, offset in zip(limits, offsets):
        layout_live |= (slot >= offset) & (slot < offset + limit)
    live = jnp.concatenate(
        [
            part.astype(jnp.int32)
            for part in (
                column >= half - shared_ref[0, 0], column < shared_ref[0, 1], layout_live
            )
        ],
        axis=1,
    ) > 0

    def scores_of(head):
        low, high, first, last = head_span(head, width)
        query = jnp.where(head_mask(head, rows, width), q_ref[:, first:last], jnp.bfloat16(0))
        product = lax.dot_general(
            query, key_ref[:used, first - begin : last - begin], NT,
            preferred_element_type=jnp.float32,
        )
        return jnp.where(live, product * scale, DEAD)

    done = begin
    if carry_ref is not None:
        mixed_ref[:, 0:LANES] = carry_ref[...]
        done = begin + LANES
    scores = scores_of(heads[0])
    for head in range(*heads):
        following = scores_of(head + 1) if head + 1 < heads[1] else None
        low, high, first, last = head_span(head, width)
        weights = jnp.exp2(scores - over_lanes(jnp.max, jnp.maximum, [scores]))
        total = over_lanes(jnp.sum, jnp.add, [weights])
        mixed = jnp.dot(
            weights.astype(jnp.bfloat16), value_ref[:used, first - begin : last - begin],
            preferred_element_type=jnp.float32,
        )
        mixed = jnp.where(head_mask(head, rows, width), mixed * (1.0 / total), 0.0)
        for at in range(first, last, LANES):
            part = mixed[:, at - first : at - first + LANES]
            if at < done:
                mixed_ref[:, at - begin : at - begin + LANES] += part
            else:
                mixed_ref[:, at - begin : at - begin + LANES] = part
                done = at + LANES
        scores = following
    size = finish - begin if last_step else out_ref.shape[1]
    state = (
        hidden_ref[:, begin : begin + size].astype(jnp.float32) + mixed_ref[:, :size]
    ).astype(jnp.bfloat16)
    if last_step:
        state_ref[...] = state
        moves[-1].start()
        for move in moves:
            move.wait()
    else:
        out_ref[...] = state
    if not last_step:
        rest[1][...] = mixed_ref[:, size : size + LANES]


def cond_attention(half, step, scalars, queries, hidden, layout, kv_parts, finished, carry):
    tokens, width = queries.shape
    heads = HEAD_STEPS[step], HEAD_STEPS[step + 1]
    cuts = column_cuts(width)
    last_step = heads[1] == HEADS
    begin = head_span(heads[0], width)[2]
    read = head_span(heads[1] - 1, width)[3]
    size = width if last_step else heads[1] * (width // HEADS) // LANES * LANES - begin
    smem = pl.BlockSpec(memory_space=pltpu.SMEM)

    def rows_of(columns):
        return pl.BlockSpec((tokens, columns), lambda i: (i, 0))

    flat = [array for pair in kv_parts for array in pair]
    operands = [*scalars, queries, hidden, *layout, *flat]
    specs = [smem, smem, rows_of(read), rows_of(read)]
    specs += [pl.BlockSpec(memory_space=pltpu.VMEM) for _ in (*layout, *flat)]
    slots = layout[0].shape[0]
    padded = LIVE_LAYOUT + (ALIGN - 1) * len(layout)
    keys = 2 * flat[0].shape[0] + -(-padded // slots) * slots + slots
    if last_step:
        operands += finished
        specs += [rows_of(array.shape[1]) for array in finished]
    if carry is not None:
        operands.append(carry)
        specs.append(rows_of(LANES))
    out_specs = [pl.BlockSpec(memory_space=pltpu.HBM) if last_step else rows_of(size)]
    out_shape = [jax.ShapeDtypeStruct((tokens, size), jnp.bfloat16)]
    if last_step:
        out_shape = [pltpu.HBM((tokens, size), jnp.bfloat16)]
    else:
        out_specs.append(rows_of(LANES))
        out_shape.append(jax.ShapeDtypeStruct((tokens, LANES), jnp.float32))
    return pl.pallas_call(
        functools.partial(cond_kernel, half, width, heads, cuts, len(kv_parts)),
        grid=(1,),
        in_specs=specs,
        out_specs=out_specs,
        out_shape=out_shape,
        scratch_shapes=[
            pltpu.VMEM((tokens, read - begin), jnp.float32),
            pltpu.VMEM((keys, read - begin), jnp.bfloat16),
            pltpu.VMEM((keys, read - begin), jnp.bfloat16),
            pltpu.VMEM((tokens, width - begin if last_step else LANES), jnp.bfloat16),
            pltpu.SemaphoreType.DMA((len(HEAD_STEPS) - 1,)),
        ],
        compiler_params=pltpu.CompilerParams(vmem_limit_bytes=VMEM_LIMIT),
        name="cond_attention",
    )(*operands)


def temporal_kernel(
    x_ref, gain_ref, w_ref, out_ref, normed_ref, qkv_ref
):
    frames, positions, width = out_ref.shape
    group = 16
    rows = frames * group
    scale = LOG2E / math.sqrt(width // HEADS)
    step = pl.program_id(0)

    @pl.when(step == 0)
    def _():
        for at in range(0, positions, group):
            state = x_ref[:, at : at + group, :].reshape(rows, width).astype(jnp.float32)
            inverse = lax.rsqrt(jnp.mean(state * state, axis=1, keepdims=True) + EPSILON)
            normed_ref[at * frames : at * frames + rows, :] = (
                state * inverse * gain_ref[...]
            ).astype(jnp.bfloat16)

    for part in range(3):

        @pl.when(step == part)
        def _():
            qkv_ref[:, part * width : (part + 1) * width] = jnp.dot(
                normed_ref[...], w_ref[...], preferred_element_type=jnp.float32
            ).astype(jnp.bfloat16)

    @pl.when(step == 2)
    def _():
        row = lax.broadcasted_iota(jnp.int32, (rows, rows), 0)
        column = lax.broadcasted_iota(jnp.int32, (rows, rows), 1)
        same = lax.rem(row, group) == lax.rem(column, group)

        def scores_of(at, head):
            low, high, first, last = head_span(head, width)
            span = slice(at * frames, at * frames + rows)
            query = jnp.where(
                head_mask(head, rows, width), qkv_ref[span, first:last], jnp.bfloat16(0)
            )
            key = qkv_ref[span, width + first : width + last]
            score = lax.dot_general(query, key, NT, preferred_element_type=jnp.float32)
            return jnp.where(same, score * scale, DEAD)

        turns = [(at, head) for at in range(0, positions, group) for head in range(HEADS)]
        tiles = {}
        score = scores_of(*turns[0])
        for turn, (at, head) in enumerate(turns):
            following = scores_of(*turns[turn + 1]) if turn + 1 < len(turns) else None
            low, high, first, last = head_span(head, width)
            span = slice(at * frames, at * frames + rows)
            weight = jnp.exp2(score - over_lanes(jnp.max, jnp.maximum, [score]))
            total = over_lanes(jnp.sum, jnp.add, [weight])
            mixed = jnp.dot(
                weight.astype(jnp.bfloat16),
                qkv_ref[span, 2 * width + first : 2 * width + last],
                preferred_element_type=jnp.float32,
            )
            mixed = jnp.where(head_mask(head, rows, width), mixed * (1.0 / total), 0.0)
            for tile in range(first, last, LANES):
                part = mixed[:, tile - first : tile - first + LANES]
                tiles[tile] = tiles[tile] + part if tile in tiles else part
                if high >= tile + LANES:
                    out_ref[:, at : at + group, tile : tile + LANES] = (
                        tiles.pop(tile).astype(jnp.bfloat16).reshape(frames, group, LANES)
                    )
            score = following


def temporal_attention(regrouped, norm_gain, w_qkv):
    frames, positions, width = regrouped.shape
    whole = pl.BlockSpec(regrouped.shape, lambda i: (0, 0, 0))
    return pl.pallas_call(
        temporal_kernel,
        grid=(3,),
        in_specs=[
            whole,
            pl.BlockSpec((1, width), lambda i: (0, 0)),
            pl.BlockSpec((width, width), lambda i: (0, i)),
        ],
        out_specs=whole,
        out_shape=jax.ShapeDtypeStruct((frames, positions, width), jnp.bfloat16),
        scratch_shapes=[
            pltpu.VMEM((frames * positions, width), jnp.bfloat16),
            pltpu.VMEM((frames * positions, 3 * width), jnp.bfloat16),
        ],
        compiler_params=pltpu.CompilerParams(vmem_limit_bytes=VMEM_LIMIT),
        name="temporal_attention",
    )(
        regrouped,
        norm_gain.reshape(1, width),
        pltpu.with_memory_space_constraint(w_qkv, pltpu.HBM),
    )


def split_kernel(half, cuts, kv_ref, *refs):
    out_refs, sems = refs[:-1], refs[-1]
    width = kv_ref.shape[2] // 2
    copies = []
    for piece, (start, end) in enumerate(zip(cuts, cuts[1:])):
        size = end - start
        for side, columns in enumerate((slice(half, 2 * half), slice(0, half))):
            out_ref = out_refs[2 * piece + side]
            for part in range(2):
                low = part * width + start
                copies.append(
                    pltpu.make_async_copy(
                        kv_ref.at[:, columns, low : low + size],
                        out_ref.at[:, :, part * size : (part + 1) * size],
                        sems.at[len(copies)],
                    )
                )
    for copy in copies:
        copy.start()
    for copy in copies:
        copy.wait()


def split_halves(own, cuts):
    rows, columns = own.shape[:2]
    shapes = [
        jax.ShapeDtypeStruct((rows, columns // 2, 2 * (end - start)), own.dtype)
        for start, end in zip(cuts, cuts[1:])
        for _ in range(2)
    ]
    local = pl.BlockSpec(memory_space=pltpu.VMEM)
    pieces = pl.pallas_call(
        functools.partial(split_kernel, columns // 2, cuts),
        in_specs=[pl.BlockSpec(memory_space=pltpu.HBM)],
        out_specs=[local] * len(shapes),
        out_shape=shapes,
        scratch_shapes=[pltpu.SemaphoreType.DMA((2 * len(shapes),))],
        compiler_params=pltpu.CompilerParams(vmem_limit_bytes=VMEM_LIMIT),
        name="split_halves",
    )(own)
    return list(zip(pieces[0::2], pieces[1::2]))


def exchange(array, axis, flip):
    length = lax.axis_size(axis)
    return lax.ppermute(array, axis, [(i, i ^ flip) for i in range(length)])


def passed_along(array, axis, by):
    length = lax.axis_size(axis)
    return lax.ppermute(array, axis, [(i, (i + by) % length) for i in range(length)])


def regroup(array):
    return lax.all_to_all(array, "frame", split_axis=0, concat_axis=0, tiled=True)


def per_device(
    hidden, cond_queries, cond_kv, layout_kv, layout_count, intersection, norm_gain, w_qkv
):
    patch_rows, patch_cols, width = hidden.shape[2:]
    half = patch_cols // 2
    tokens = patch_rows * patch_cols
    frames = lax.axis_size("frame")
    cuts = column_cuts(width)
    own = pltpu.with_memory_space_constraint(cond_kv[0, 0], pltpu.HBM)

    def sent(pair):
        return tuple(
            passed_along(side, "view", by).reshape(patch_rows * half, -1)
            for side, by in zip(pair, (1, -1))
        )

    layout = layout_kv[0]
    (first_source,) = split_halves(own, cuts[:2])
    first = sent(first_source)
    across = exchange(layout, "band", 2)
    beside = exchange(layout, "band", 1)
    sources, across = lax.optimization_barrier((split_halves(own, cuts[1:]), across))
    diagonal = exchange(across, "band", 1)
    second = sent(sources[0])
    last_source, first = lax.optimization_barrier((sources[1], first))
    kv_parts = [first, second, sent(last_source)]
    layout = (layout, beside, across, diagonal)
    scalars = (layout_count, intersection)
    queries = cond_queries[0, 0].reshape(tokens, width)
    hidden_rows = hidden[0, 0].reshape(tokens, width)
    finished, carry = [], None
    for step in range(len(kv_parts)):
        result = cond_attention(
            half, step, scalars, queries, hidden_rows, layout, kv_parts[: step + 1],
            finished, carry,
        )
        finished, carry = finished + [result[0]], result[-1]
    regrouped = regroup(finished[-1].reshape(frames, -1, width))
    output = regroup(temporal_attention(regrouped, norm_gain, w_qkv))
    return output.reshape(1, 1, patch_rows, patch_cols, width)


def solution(mesh):
    in_specs = (
        P("view", "frame", "band", None, None),
        P("view", "frame", "band", None, None),
        P("view", "frame", "band", None, None),
        P("frame", "band", None),
        P("frame", None),
        P("view", None),
        P(),
        P(),
    )
    out_specs = P("view", "frame", "band", None, None)
    return jax.shard_map(
        per_device, mesh=mesh, in_specs=in_specs, out_specs=out_specs, check_vma=False
    )
```

```python
import functools
import math

import jax
import jax.numpy as jnp
from jax import lax
from jax.experimental import pallas as pl
from jax.experimental.pallas import tpu as pltpu
from jax.sharding import PartitionSpec as P

HEADS = 16
LANES = 128
HEAD_STEPS = (0, 8, 12, 16)
EPSILON = 1e-06
DEAD = -1e30
VMEM_LIMIT = 32 << 20
LIVE_LAYOUT = 320
ALIGN = 16
LOG2E = 1.4426950408889634
NT = (((1,), (1,)), ((), ()))


def head_span(head, width):
    size = width // HEADS
    low, high = head * size, (head + 1) * size
    return low, high, low // LANES * LANES, -(-high // LANES) * LANES


def head_mask(head, rows, width):
    low, high, first, last = head_span(head, width)
    column = lax.broadcasted_iota(jnp.int32, (rows, last - first), 1) + first
    return (column >= low) & (column < high)


def lane_index(count):
    return lax.broadcasted_iota(jnp.int32, (1, count), 1)


def over_lanes(reduce_lanes, combine, pieces):
    tiles = [
        piece[:, at : at + LANES] for piece in pieces for at in range(0, piece.shape[1], LANES)
    ]
    while len(tiles) > 1:
        pairs = [combine(a, b) for a, b in zip(tiles[0::2], tiles[1::2])]
        tiles = pairs + tiles[len(tiles) // 2 * 2 :]
    return reduce_lanes(tiles[0], axis=1, keepdims=True)


def column_cuts(width):
    return (0, *(head_span(end - 1, width)[3] for end in HEAD_STEPS[1:]))


def cond_kernel(half, width, heads, cuts, count_kv, *refs):
    count_ref, shared_ref, q_ref, hidden_ref = refs[:4]
    layout_refs = refs[4:8]
    kv_refs = refs[8 : 8 + 2 * count_kv]
    rest = list(refs[8 + 2 * count_kv :])
    mixed_ref, key_ref, value_ref, state_ref, sems = rest[-5:]
    last_step = heads[1] == HEADS
    finished = []
    if last_step:
        finished, rest = rest[: count_kv - 1], rest[count_kv - 1 :]
    carry_ref = rest.pop(0) if heads[0] > 0 else None
    out_ref = rest[0]
    rows = q_ref.shape[0]
    scale = LOG2E / math.sqrt(width // HEADS)
    begin = head_span(heads[0], width)[2]
    finish = head_span(heads[1] - 1, width)[3]
    keys = kv_refs[0].shape[0]
    slots = layout_refs[0].shape[0]

    moves = []
    if last_step:
        at = 0
        for ref in finished:
            columns = slice(at, at + ref.shape[1])
            moves.append(pltpu.make_async_copy(ref, out_ref.at[:, columns], sems.at[len(moves)]))
            at += ref.shape[1]
        for move in moves:
            move.start()

    band = lax.axis_index("band")
    limits = [count_ref[0, jnp.bitwise_xor(band, block)] for block in range(len(layout_refs))]
    offsets = [2 * keys]
    for limit in limits:
        offsets.append(offsets[-1] + (limit + ALIGN - 1) // ALIGN * ALIGN)

    for target, shift in ((key_ref, 0), (value_ref, 1)):
        for part in range(count_kv):
            start, end = max(cuts[part], begin), min(cuts[part + 1], finish)
            size = cuts[part + 1] - cuts[part]
            low = start - cuts[part] + shift * size
            for side in range(2 if start < end else 0):
                target[side * keys : (side + 1) * keys, start - begin : end - begin] = (
                    kv_refs[2 * part + side][:, low : low + end - start]
                )
        low = shift * width + begin
        spare = key_ref.shape[0] - slots
        columns = slice(low, low + finish - begin)
        for at in range(2 * keys, spare, slots):
            target[at : at + slots, :] = layout_refs[0][:, columns]
        for ref, offset in zip(layout_refs, offsets):
            at = pl.multiple_of(offset, ALIGN)
            target[pl.ds(at, slots), :] = ref[:, columns]

    used = key_ref.shape[0] - slots
    column = lax.rem(lane_index(keys), half)
    slot = lane_index(used - 2 * keys) + 2 * keys
    layout_live = slot < 0
    for limit, offset in zip(limits, offsets):
        layout_live |= (slot >= offset) & (slot < offset + limit)
    live = jnp.concatenate(
        [
            part.astype(jnp.int32)
            for part in (
                column >= half - shared_ref[0, 0], column < shared_ref[0, 1], layout_live
            )
        ],
        axis=1,
    ) > 0

    def scores_of(head):
        low, high, first, last = head_span(head, width)
        query = jnp.where(head_mask(head, rows, width), q_ref[:, first:last], jnp.bfloat16(0))
        product = lax.dot_general(
            query, key_ref[:used, first - begin : last - begin], NT,
            preferred_element_type=jnp.float32,
        )
        return jnp.where(live, product * scale, DEAD)

    done = begin
    if carry_ref is not None:
        mixed_ref[:, 0:LANES] = carry_ref[...]
        done = begin + LANES
    scores = scores_of(heads[0])
    for head in range(*heads):
        following = scores_of(head + 1) if head + 1 < heads[1] else None
        low, high, first, last = head_span(head, width)
        weights = jnp.exp2(scores - over_lanes(jnp.max, jnp.maximum, [scores]))
        total = over_lanes(jnp.sum, jnp.add, [weights])
        mixed = jnp.dot(
            weights.astype(jnp.bfloat16), value_ref[:used, first - begin : last - begin],
            preferred_element_type=jnp.float32,
        )
        mixed = jnp.where(head_mask(head, rows, width), mixed * (1.0 / total), 0.0)
        for at in range(first, last, LANES):
            part = mixed[:, at - first : at - first + LANES]
            if at < done:
                mixed_ref[:, at - begin : at - begin + LANES] += part
            else:
                mixed_ref[:, at - begin : at - begin + LANES] = part
                done = at + LANES
            if last_step and high >= at + LANES:
                tile = slice(at - begin, at - begin + LANES)
                state_ref[:, tile] = (
                    hidden_ref[:, at : at + LANES].astype(jnp.float32) + mixed_ref[:, tile]
                ).astype(jnp.bfloat16)
                moves.append(
                    pltpu.make_async_copy(
                        state_ref.at[:, tile], out_ref.at[:, at : at + LANES],
                        sems.at[len(moves)],
                    )
                )
                moves[-1].start()
        scores = following
    if last_step:
        for move in moves:
            move.wait()
    else:
        size = out_ref.shape[1]
        out_ref[...] = (
            hidden_ref[:, begin : begin + size].astype(jnp.float32) + mixed_ref[:, :size]
        ).astype(jnp.bfloat16)
    if not last_step:
        rest[1][...] = mixed_ref[:, size : size + LANES]


def cond_attention(half, step, scalars, queries, hidden, layout, kv_parts, finished, carry):
    tokens, width = queries.shape
    heads = HEAD_STEPS[step], HEAD_STEPS[step + 1]
    cuts = column_cuts(width)
    last_step = heads[1] == HEADS
    begin = head_span(heads[0], width)[2]
    read = head_span(heads[1] - 1, width)[3]
    size = width if last_step else heads[1] * (width // HEADS) // LANES * LANES - begin
    smem = pl.BlockSpec(memory_space=pltpu.SMEM)

    def rows_of(columns):
        return pl.BlockSpec((tokens, columns), lambda i: (i, 0))

    flat = [array for pair in kv_parts for array in pair]
    operands = [*scalars, queries, hidden, *layout, *flat]
    specs = [smem, smem, rows_of(read), rows_of(read)]
    specs += [pl.BlockSpec(memory_space=pltpu.VMEM) for _ in (*layout, *flat)]
    slots = layout[0].shape[0]
    padded = LIVE_LAYOUT + (ALIGN - 1) * len(layout)
    keys = 2 * flat[0].shape[0] + -(-padded // slots) * slots + slots
    if last_step:
        operands += finished
        specs += [rows_of(array.shape[1]) for array in finished]
    if carry is not None:
        operands.append(carry)
        specs.append(rows_of(LANES))
    out_specs = [pl.BlockSpec(memory_space=pltpu.HBM) if last_step else rows_of(size)]
    out_shape = [jax.ShapeDtypeStruct((tokens, size), jnp.bfloat16)]
    if last_step:
        out_shape = [pltpu.HBM((tokens, size), jnp.bfloat16)]
    else:
        out_specs.append(rows_of(LANES))
        out_shape.append(jax.ShapeDtypeStruct((tokens, LANES), jnp.float32))
    return pl.pallas_call(
        functools.partial(cond_kernel, half, width, heads, cuts, len(kv_parts)),
        grid=(1,),
        in_specs=specs,
        out_specs=out_specs,
        out_shape=out_shape,
        scratch_shapes=[
            pltpu.VMEM((tokens, read - begin), jnp.float32),
            pltpu.VMEM((keys, read - begin), jnp.bfloat16),
            pltpu.VMEM((keys, read - begin), jnp.bfloat16),
            pltpu.VMEM((tokens, width - begin if last_step else LANES), jnp.bfloat16),
            pltpu.SemaphoreType.DMA((len(finished) + (width - begin) // LANES,)),
        ],
        compiler_params=pltpu.CompilerParams(vmem_limit_bytes=VMEM_LIMIT),
        name="cond_attention",
    )(*operands)


def temporal_kernel(
    x_ref, gain_ref, w_ref, out_ref, normed_ref, qkv_ref
):
    frames, positions, width = out_ref.shape
    group = 16
    rows = frames * group
    scale = LOG2E / math.sqrt(width // HEADS)
    step = pl.program_id(0)

    @pl.when(step == 0)
    def _():
        for at in range(0, positions, group):
            state = x_ref[:, at : at + group, :].reshape(rows, width).astype(jnp.float32)
            inverse = lax.rsqrt(jnp.mean(state * state, axis=1, keepdims=True) + EPSILON)
            normed_ref[at * frames : at * frames + rows, :] = (
                state * inverse * gain_ref[...]
            ).astype(jnp.bfloat16)

    for part in range(3):

        @pl.when(step == part)
        def _():
            qkv_ref[:, part * width : (part + 1) * width] = jnp.dot(
                normed_ref[...], w_ref[...], preferred_element_type=jnp.float32
            ).astype(jnp.bfloat16)

    @pl.when(step == 2)
    def _():
        row = lax.broadcasted_iota(jnp.int32, (rows, rows), 0)
        column = lax.broadcasted_iota(jnp.int32, (rows, rows), 1)
        same = lax.rem(row, group) == lax.rem(column, group)

        def scores_of(at, head):
            low, high, first, last = head_span(head, width)
            span = slice(at * frames, at * frames + rows)
            query = jnp.where(
                head_mask(head, rows, width), qkv_ref[span, first:last], jnp.bfloat16(0)
            )
            key = qkv_ref[span, width + first : width + last]
            score = lax.dot_general(query, key, NT, preferred_element_type=jnp.float32)
            return jnp.where(same, score * scale, DEAD)

        turns = [(at, head) for at in range(0, positions, group) for head in range(HEADS)]
        tiles = {}
        score = scores_of(*turns[0])
        for turn, (at, head) in enumerate(turns):
            following = scores_of(*turns[turn + 1]) if turn + 1 < len(turns) else None
            low, high, first, last = head_span(head, width)
            span = slice(at * frames, at * frames + rows)
            weight = jnp.exp2(score - over_lanes(jnp.max, jnp.maximum, [score]))
            total = over_lanes(jnp.sum, jnp.add, [weight])
            mixed = jnp.dot(
                weight.astype(jnp.bfloat16),
                qkv_ref[span, 2 * width + first : 2 * width + last],
                preferred_element_type=jnp.float32,
            )
            mixed = jnp.where(head_mask(head, rows, width), mixed * (1.0 / total), 0.0)
            for tile in range(first, last, LANES):
                part = mixed[:, tile - first : tile - first + LANES]
                tiles[tile] = tiles[tile] + part if tile in tiles else part
                if high >= tile + LANES:
                    out_ref[:, at : at + group, tile : tile + LANES] = (
                        tiles.pop(tile).astype(jnp.bfloat16).reshape(frames, group, LANES)
                    )
            score = following


def temporal_attention(regrouped, norm_gain, w_qkv):
    frames, positions, width = regrouped.shape
    whole = pl.BlockSpec(regrouped.shape, lambda i: (0, 0, 0))
    return pl.pallas_call(
        temporal_kernel,
        grid=(3,),
        in_specs=[
            whole,
            pl.BlockSpec((1, width), lambda i: (0, 0)),
            pl.BlockSpec((width, width), lambda i: (0, i)),
        ],
        out_specs=whole,
        out_shape=jax.ShapeDtypeStruct((frames, positions, width), jnp.bfloat16),
        scratch_shapes=[
            pltpu.VMEM((frames * positions, width), jnp.bfloat16),
            pltpu.VMEM((frames * positions, 3 * width), jnp.bfloat16),
        ],
        compiler_params=pltpu.CompilerParams(vmem_limit_bytes=VMEM_LIMIT),
        name="temporal_attention",
    )(
        regrouped,
        norm_gain.reshape(1, width),
        pltpu.with_memory_space_constraint(w_qkv, pltpu.HBM),
    )


def split_kernel(half, cuts, kv_ref, *refs):
    out_refs, sems = refs[:-1], refs[-1]
    width = kv_ref.shape[2] // 2
    copies = []
    for piece, (start, end) in enumerate(zip(cuts, cuts[1:])):
        size = end - start
        for side, columns in enumerate((slice(half, 2 * half), slice(0, half))):
            out_ref = out_refs[2 * piece + side]
            for part in range(2):
                low = part * width + start
                copies.append(
                    pltpu.make_async_copy(
                        kv_ref.at[:, columns, low : low + size],
                        out_ref.at[:, :, part * size : (part + 1) * size],
                        sems.at[len(copies)],
                    )
                )
    for copy in copies:
        copy.start()
    for copy in copies:
        copy.wait()


def split_halves(own, cuts):
    rows, columns = own.shape[:2]
    shapes = [
        jax.ShapeDtypeStruct((rows, columns // 2, 2 * (end - start)), own.dtype)
        for start, end in zip(cuts, cuts[1:])
        for _ in range(2)
    ]
    local = pl.BlockSpec(memory_space=pltpu.VMEM)
    pieces = pl.pallas_call(
        functools.partial(split_kernel, columns // 2, cuts),
        in_specs=[pl.BlockSpec(memory_space=pltpu.HBM)],
        out_specs=[local] * len(shapes),
        out_shape=shapes,
        scratch_shapes=[pltpu.SemaphoreType.DMA((2 * len(shapes),))],
        compiler_params=pltpu.CompilerParams(vmem_limit_bytes=VMEM_LIMIT),
        name="split_halves",
    )(own)
    return list(zip(pieces[0::2], pieces[1::2]))


def exchange(array, axis, flip):
    length = lax.axis_size(axis)
    return lax.ppermute(array, axis, [(i, i ^ flip) for i in range(length)])


def passed_along(array, axis, by):
    length = lax.axis_size(axis)
    return lax.ppermute(array, axis, [(i, (i + by) % length) for i in range(length)])


def regroup(array):
    return lax.all_to_all(array, "frame", split_axis=0, concat_axis=0, tiled=True)


def per_device(
    hidden, cond_queries, cond_kv, layout_kv, layout_count, intersection, norm_gain, w_qkv
):
    patch_rows, patch_cols, width = hidden.shape[2:]
    half = patch_cols // 2
    tokens = patch_rows * patch_cols
    frames = lax.axis_size("frame")
    cuts = column_cuts(width)
    own = pltpu.with_memory_space_constraint(cond_kv[0, 0], pltpu.HBM)

    def sent(pair):
        return tuple(
            passed_along(side, "view", by).reshape(patch_rows * half, -1)
            for side, by in zip(pair, (1, -1))
        )

    layout = layout_kv[0]
    (first_source,) = split_halves(own, cuts[:2])
    first = sent(first_source)
    across = exchange(layout, "band", 2)
    beside = exchange(layout, "band", 1)
    sources, across = lax.optimization_barrier((split_halves(own, cuts[1:]), across))
    diagonal = exchange(across, "band", 1)
    second = sent(sources[0])
    last_source, first = lax.optimization_barrier((sources[1], first))
    kv_parts = [first, second, sent(last_source)]
    layout = (layout, beside, across, diagonal)
    scalars = (layout_count, intersection)
    queries = cond_queries[0, 0].reshape(tokens, width)
    hidden_rows = hidden[0, 0].reshape(tokens, width)
    finished, carry = [], None
    for step in range(len(kv_parts)):
        result = cond_attention(
            half, step, scalars, queries, hidden_rows, layout, kv_parts[: step + 1],
            finished, carry,
        )
        finished, carry = finished + [result[0]], result[-1]
    regrouped = regroup(finished[-1].reshape(frames, -1, width))
    output = regroup(temporal_attention(regrouped, norm_gain, w_qkv))
    return output.reshape(1, 1, patch_rows, patch_cols, width)


def solution(mesh):
    in_specs = (
        P("view", "frame", "band", None, None),
        P("view", "frame", "band", None, None),
        P("view", "frame", "band", None, None),
        P("frame", "band", None),
        P("frame", None),
        P("view", None),
        P(),
        P(),
    )
    out_specs = P("view", "frame", "band", None, None)
    return jax.shard_map(
        per_device, mesh=mesh, in_specs=in_specs, out_specs=out_specs, check_vma=False
    )
```

```python
import functools
import math

import jax
import jax.numpy as jnp
from jax import lax
from jax.experimental import pallas as pl
from jax.experimental.pallas import tpu as pltpu
from jax.sharding import PartitionSpec as P

HEADS = 16
LANES = 128
HEAD_STEPS = (0, 8, 12, 16)
EPSILON = 1e-06
DEAD = -1e30
VMEM_LIMIT = 32 << 20
LIVE_LAYOUT = 320
ALIGN = 16
LOG2E = 1.4426950408889634
NT = (((1,), (1,)), ((), ()))


def head_span(head, width):
    size = width // HEADS
    low, high = head * size, (head + 1) * size
    return low, high, low // LANES * LANES, -(-high // LANES) * LANES


def head_mask(head, rows, width):
    low, high, first, last = head_span(head, width)
    column = lax.broadcasted_iota(jnp.int32, (rows, last - first), 1) + first
    return (column >= low) & (column < high)


def lane_index(count):
    return lax.broadcasted_iota(jnp.int32, (1, count), 1)


def over_lanes(reduce_lanes, combine, pieces):
    tiles = [
        piece[:, at : at + LANES] for piece in pieces for at in range(0, piece.shape[1], LANES)
    ]
    while len(tiles) > 1:
        pairs = [combine(a, b) for a, b in zip(tiles[0::2], tiles[1::2])]
        tiles = pairs + tiles[len(tiles) // 2 * 2 :]
    return reduce_lanes(tiles[0], axis=1, keepdims=True)


def column_cuts(width):
    return (0, *(head_span(end - 1, width)[3] for end in HEAD_STEPS[1:]))


def cond_kernel(half, width, heads, cuts, count_kv, *refs):
    count_ref, shared_ref, q_ref, hidden_ref = refs[:4]
    layout_refs = refs[4:8]
    kv_refs = refs[8 : 8 + 2 * count_kv]
    rest = list(refs[8 + 2 * count_kv :])
    mixed_ref, key_ref, value_ref, state_ref, sems = rest[-5:]
    last_step = heads[1] == HEADS
    finished = []
    if last_step:
        finished, rest = rest[: count_kv - 1], rest[count_kv - 1 :]
    carry_ref = rest.pop(0) if heads[0] > 0 else None
    out_ref = rest[0]
    rows = q_ref.shape[0]
    scale = LOG2E / math.sqrt(width // HEADS)
    begin = head_span(heads[0], width)[2]
    finish = head_span(heads[1] - 1, width)[3]
    keys = kv_refs[0].shape[0]
    slots = layout_refs[0].shape[0]

    moves = []
    if last_step:
        at = 0
        for ref in finished:
            columns = slice(at, at + ref.shape[1])
            moves.append(pltpu.make_async_copy(ref, out_ref.at[:, columns], sems.at[len(moves)]))
            at += ref.shape[1]
        for move in moves:
            move.start()

    band = lax.axis_index("band")
    limits = [count_ref[0, jnp.bitwise_xor(band, block)] for block in range(len(layout_refs))]
    offsets = [2 * keys]
    for limit in limits:
        offsets.append(offsets[-1] + (limit + ALIGN - 1) // ALIGN * ALIGN)

    for target, shift in ((key_ref, 0), (value_ref, 1)):
        for part in range(count_kv):
            start, end = max(cuts[part], begin), min(cuts[part + 1], finish)
            size = cuts[part + 1] - cuts[part]
            low = start - cuts[part] + shift * size
            for side in range(2 if start < end else 0):
                target[side * keys : (side + 1) * keys, start - begin : end - begin] = (
                    kv_refs[2 * part + side][:, low : low + end - start]
                )
        low = shift * width + begin
        spare = key_ref.shape[0] - slots
        columns = slice(low, low + finish - begin)
        for at in range(2 * keys, spare, slots):
            target[at : at + slots, :] = layout_refs[0][:, columns]
        for ref, offset in zip(layout_refs, offsets):
            at = pl.multiple_of(offset, ALIGN)
            target[pl.ds(at, slots), :] = ref[:, columns]

    used = key_ref.shape[0] - slots
    column = lax.rem(lane_index(keys), half)
    slot = lane_index(used - 2 * keys) + 2 * keys
    layout_live = slot < 0
    for limit, offset in zip(limits, offsets):
        layout_live |= (slot >= offset) & (slot < offset + limit)
    live = jnp.concatenate(
        [
            part.astype(jnp.int32)
            for part in (
                column >= half - shared_ref[0, 0], column < shared_ref[0, 1], layout_live
            )
        ],
        axis=1,
    ) > 0

    def scores_of(head):
        low, high, first, last = head_span(head, width)
        query = jnp.where(head_mask(head, rows, width), q_ref[:, first:last], jnp.bfloat16(0))
        product = lax.dot_general(
            query, key_ref[:used, first - begin : last - begin], NT,
            preferred_element_type=jnp.float32,
        )
        return jnp.where(live, product * scale, DEAD)

    done = begin
    if carry_ref is not None:
        mixed_ref[:, 0:LANES] = carry_ref[...]
        done = begin + LANES
    scores = scores_of(heads[0])
    for head in range(*heads):
        following = scores_of(head + 1) if head + 1 < heads[1] else None
        low, high, first, last = head_span(head, width)
        weights = jnp.exp2(scores - over_lanes(jnp.max, jnp.maximum, [scores]))
        total = over_lanes(jnp.sum, jnp.add, [weights])
        mixed = jnp.dot(
            weights.astype(jnp.bfloat16), value_ref[:used, first - begin : last - begin],
            preferred_element_type=jnp.float32,
        )
        mixed = jnp.where(head_mask(head, rows, width), mixed * (1.0 / total), 0.0)
        for at in range(first, last, LANES):
            part = mixed[:, at - first : at - first + LANES]
            if at < done:
                mixed_ref[:, at - begin : at - begin + LANES] += part
            else:
                mixed_ref[:, at - begin : at - begin + LANES] = part
                done = at + LANES
            if last_step and high >= at + LANES:
                tile = slice(at - begin, at - begin + LANES)
                state_ref[:, tile] = (
                    hidden_ref[:, at : at + LANES].astype(jnp.float32) + mixed_ref[:, tile]
                ).astype(jnp.bfloat16)
                moves.append(
                    pltpu.make_async_copy(
                        state_ref.at[:, tile], out_ref.at[:, at : at + LANES],
                        sems.at[len(moves)],
                    )
                )
                moves[-1].start()
        scores = following
    if last_step:
        for move in moves:
            move.wait()
    else:
        size = out_ref.shape[1]
        out_ref[...] = (
            hidden_ref[:, begin : begin + size].astype(jnp.float32) + mixed_ref[:, :size]
        ).astype(jnp.bfloat16)
    if not last_step:
        rest[1][...] = mixed_ref[:, size : size + LANES]


def cond_attention(half, step, scalars, queries, hidden, layout, kv_parts, finished, carry):
    tokens, width = queries.shape
    heads = HEAD_STEPS[step], HEAD_STEPS[step + 1]
    cuts = column_cuts(width)
    last_step = heads[1] == HEADS
    begin = head_span(heads[0], width)[2]
    read = head_span(heads[1] - 1, width)[3]
    size = width if last_step else heads[1] * (width // HEADS) // LANES * LANES - begin
    smem = pl.BlockSpec(memory_space=pltpu.SMEM)

    def rows_of(columns):
        return pl.BlockSpec((tokens, columns), lambda i: (i, 0))

    flat = [array for pair in kv_parts for array in pair]
    operands = [*scalars, queries, hidden, *layout, *flat]
    specs = [smem, smem, rows_of(read), rows_of(read)]
    specs += [pl.BlockSpec(memory_space=pltpu.VMEM) for _ in (*layout, *flat)]
    slots = layout[0].shape[0]
    padded = LIVE_LAYOUT + (ALIGN - 1) * len(layout)
    keys = 2 * flat[0].shape[0] + -(-padded // slots) * slots + slots
    if last_step:
        operands += finished
        specs += [rows_of(array.shape[1]) for array in finished]
    if carry is not None:
        operands.append(carry)
        specs.append(rows_of(LANES))
    out_specs = [pl.BlockSpec(memory_space=pltpu.HBM) if last_step else rows_of(size)]
    out_shape = [jax.ShapeDtypeStruct((tokens, size), jnp.bfloat16)]
    if last_step:
        out_shape = [pltpu.HBM((tokens, size), jnp.bfloat16)]
    else:
        out_specs.append(rows_of(LANES))
        out_shape.append(jax.ShapeDtypeStruct((tokens, LANES), jnp.float32))
    return pl.pallas_call(
        functools.partial(cond_kernel, half, width, heads, cuts, len(kv_parts)),
        grid=(1,),
        in_specs=specs,
        out_specs=out_specs,
        out_shape=out_shape,
        scratch_shapes=[
            pltpu.VMEM((tokens, read - begin), jnp.float32),
            pltpu.VMEM((keys, read - begin), jnp.bfloat16),
            pltpu.VMEM((keys, read - begin), jnp.bfloat16),
            pltpu.VMEM((tokens, width - begin if last_step else LANES), jnp.bfloat16),
            pltpu.SemaphoreType.DMA((len(finished) + (width - begin) // LANES,)),
        ],
        compiler_params=pltpu.CompilerParams(vmem_limit_bytes=VMEM_LIMIT),
        name="cond_attention",
    )(*operands)


def temporal_kernel(
    x_ref, gain_ref, w_ref, out_ref, normed_ref, qkv_ref
):
    frames, positions, width = out_ref.shape
    group = 16
    rows = frames * group
    scale = LOG2E / math.sqrt(width // HEADS)
    step = pl.program_id(0)

    @pl.when(step == 0)
    def _():
        for at in range(0, positions, group):
            state = x_ref[:, at : at + group, :].reshape(rows, width).astype(jnp.float32)
            inverse = lax.rsqrt(jnp.mean(state * state, axis=1, keepdims=True) + EPSILON)
            normed_ref[at * frames : at * frames + rows, :] = (
                state * inverse * gain_ref[...]
            ).astype(jnp.bfloat16)

    for part in range(3):

        @pl.when(step == part)
        def _():
            qkv_ref[:, part * width : (part + 1) * width] = jnp.dot(
                normed_ref[...], w_ref[...], preferred_element_type=jnp.float32
            ).astype(jnp.bfloat16)

    @pl.when(step == 2)
    def _():
        row = lax.broadcasted_iota(jnp.int32, (rows, rows), 0)
        column = lax.broadcasted_iota(jnp.int32, (rows, rows), 1)
        same = lax.rem(row, group) == lax.rem(column, group)

        def scores_of(at, head):
            low, high, first, last = head_span(head, width)
            span = slice(at * frames, at * frames + rows)
            query = jnp.where(
                head_mask(head, rows, width), qkv_ref[span, first:last], jnp.bfloat16(0)
            )
            key = qkv_ref[span, width + first : width + last]
            score = lax.dot_general(query, key, NT, preferred_element_type=jnp.float32)
            return jnp.where(same, score * scale, DEAD)

        turns = [(at, head) for at in range(0, positions, group) for head in range(HEADS)]
        tiles = {}
        score = scores_of(*turns[0])
        for turn, (at, head) in enumerate(turns):
            following = scores_of(*turns[turn + 1]) if turn + 1 < len(turns) else None
            low, high, first, last = head_span(head, width)
            span = slice(at * frames, at * frames + rows)
            weight = jnp.exp2(score - over_lanes(jnp.max, jnp.maximum, [score]))
            total = over_lanes(jnp.sum, jnp.add, [weight])
            mixed = jnp.dot(
                weight.astype(jnp.bfloat16),
                qkv_ref[span, 2 * width + first : 2 * width + last],
                preferred_element_type=jnp.float32,
            )
            mixed = jnp.where(head_mask(head, rows, width), mixed * (1.0 / total), 0.0)
            for tile in range(first, last, LANES):
                part = mixed[:, tile - first : tile - first + LANES]
                tiles[tile] = tiles[tile] + part if tile in tiles else part
                if high >= tile + LANES:
                    out_ref[:, at : at + group, tile : tile + LANES] = (
                        tiles.pop(tile).astype(jnp.bfloat16).reshape(frames, group, LANES)
                    )
            score = following


def temporal_attention(regrouped, norm_gain, w_qkv):
    frames, positions, width = regrouped.shape
    whole = pl.BlockSpec(regrouped.shape, lambda i: (0, 0, 0))
    return pl.pallas_call(
        temporal_kernel,
        grid=(3,),
        in_specs=[
            whole,
            pl.BlockSpec((1, width), lambda i: (0, 0)),
            pl.BlockSpec((width, width), lambda i: (0, i)),
        ],
        out_specs=whole,
        out_shape=jax.ShapeDtypeStruct((frames, positions, width), jnp.bfloat16),
        scratch_shapes=[
            pltpu.VMEM((frames * positions, width), jnp.bfloat16),
            pltpu.VMEM((frames * positions, 3 * width), jnp.bfloat16),
        ],
        compiler_params=pltpu.CompilerParams(vmem_limit_bytes=VMEM_LIMIT),
        name="temporal_attention",
    )(
        regrouped,
        norm_gain.reshape(1, width),
        pltpu.with_memory_space_constraint(w_qkv, pltpu.HBM),
    )


def split_kernel(half, cuts, kv_ref, *refs):
    out_refs, sems = refs[:-1], refs[-1]
    width = kv_ref.shape[2] // 2
    copies = []
    for piece, (start, end) in enumerate(zip(cuts, cuts[1:])):
        size = end - start
        for side, columns in enumerate((slice(half, 2 * half), slice(0, half))):
            out_ref = out_refs[2 * piece + side]
            for part in range(2):
                low = part * width + start
                copies.append(
                    pltpu.make_async_copy(
                        kv_ref.at[:, columns, low : low + size],
                        out_ref.at[:, :, part * size : (part + 1) * size],
                        sems.at[len(copies)],
                    )
                )
    for copy in copies:
        copy.start()
    for copy in copies:
        copy.wait()


def split_halves(own, cuts):
    rows, columns = own.shape[:2]
    shapes = [
        jax.ShapeDtypeStruct((rows, columns // 2, 2 * (end - start)), own.dtype)
        for start, end in zip(cuts, cuts[1:])
        for _ in range(2)
    ]
    local = pl.BlockSpec(memory_space=pltpu.VMEM)
    pieces = pl.pallas_call(
        functools.partial(split_kernel, columns // 2, cuts),
        in_specs=[pl.BlockSpec(memory_space=pltpu.HBM)],
        out_specs=[local] * len(shapes),
        out_shape=shapes,
        scratch_shapes=[pltpu.SemaphoreType.DMA((2 * len(shapes),))],
        compiler_params=pltpu.CompilerParams(vmem_limit_bytes=VMEM_LIMIT),
        name="split_halves",
    )(own)
    return list(zip(pieces[0::2], pieces[1::2]))


def exchange(array, axis, flip):
    length = lax.axis_size(axis)
    return lax.ppermute(array, axis, [(i, i ^ flip) for i in range(length)])


def passed_along(array, axis, by):
    length = lax.axis_size(axis)
    return lax.ppermute(array, axis, [(i, (i + by) % length) for i in range(length)])


def regroup(array):
    return lax.all_to_all(array, "frame", split_axis=0, concat_axis=0, tiled=True)


def per_device(
    hidden, cond_queries, cond_kv, layout_kv, layout_count, intersection, norm_gain, w_qkv
):
    patch_rows, patch_cols, width = hidden.shape[2:]
    half = patch_cols // 2
    tokens = patch_rows * patch_cols
    frames = lax.axis_size("frame")
    cuts = column_cuts(width)
    own = pltpu.with_memory_space_constraint(cond_kv[0, 0], pltpu.HBM)

    def sent(pair):
        return tuple(
            passed_along(side, "view", by).reshape(patch_rows * half, -1)
            for side, by in zip(pair, (1, -1))
        )

    layout = layout_kv[0]
    (first_source,) = split_halves(own, cuts[:2])
    first_source, layout = lax.optimization_barrier((first_source, layout))
    first = sent(first_source)
    across = exchange(layout, "band", 2)
    beside = exchange(layout, "band", 1)
    sources, across = lax.optimization_barrier((split_halves(own, cuts[1:]), across))
    diagonal = exchange(across, "band", 1)
    second = sent(sources[0])
    last_source, first = lax.optimization_barrier((sources[1], first))
    kv_parts = [first, second, sent(last_source)]
    layout = (layout, beside, across, diagonal)
    scalars = (layout_count, intersection)
    queries = cond_queries[0, 0].reshape(tokens, width)
    hidden_rows = hidden[0, 0].reshape(tokens, width)
    finished, carry = [], None
    for step in range(len(kv_parts)):
        result = cond_attention(
            half, step, scalars, queries, hidden_rows, layout, kv_parts[: step + 1],
            finished, carry,
        )
        finished, carry = finished + [result[0]], result[-1]
    regrouped = regroup(finished[-1].reshape(frames, -1, width))
    output = regroup(temporal_attention(regrouped, norm_gain, w_qkv))
    return output.reshape(1, 1, patch_rows, patch_cols, width)


def solution(mesh):
    in_specs = (
        P("view", "frame", "band", None, None),
        P("view", "frame", "band", None, None),
        P("view", "frame", "band", None, None),
        P("frame", "band", None),
        P("frame", None),
        P("view", None),
        P(),
        P(),
    )
    out_specs = P("view", "frame", "band", None, None)
    return jax.shard_map(
        per_device, mesh=mesh, in_specs=in_specs, out_specs=out_specs, check_vma=False
    )
```
